32 devices in a mesh: seq: 16 (over z, y, x), dp: 2 (over core).
Axes of the slice: x: 2, y: 2, z: 4, core: 2. Of those that a mesh axis runs over, the one named last changes fastest.
Arguments:
- queries: bfloat16 [2, 2048, 2048], P('dp', 'seq'), may hold values from -40 to 40
- keys: bfloat16 [2, 2048, 2048], P('dp', 'seq'), may hold values from -6 to 6
- values: bfloat16 [2, 2048, 2048], P('dp', 'seq'), may hold values from -6 to 6
- grad_out: bfloat16 [2, 2048, 2048], P('dp', 'seq'), may hold values from -48 to 48
- lengths: int32 [2], P('dp'), may hold values from 256 to 2048, as said below
- fields: int32 [2, 2048], P('dp', 'seq'), may hold values from 0 to 63
- field_bias: bfloat16 [16, 64], replicated, may hold values from -6 to 6
Outputs:
- grad_queries: bfloat16 [2, 2048, 2048], P('dp', 'seq')
- grad_keys: bfloat16 [2, 2048, 2048], P('dp', 'seq')
- grad_values: bfloat16 [2, 2048, 2048], P('dp', 'seq')
- grad_bias: float32 [16, 64], replicated
The draws below stay inside these ranges and needn't reach their ends.
Inputs may be any that keep to these rules, and one draw needn't show every extreme that they name: `lengths`: the valid positions of a sequence form a prefix; in every draw some sequence is full.
All inputs are finite; a program needn't handle non-finite values.
Results may differ from the reference program's by a relative error of at most 0.0077.
Values may be sent and summed in bfloat16 or wider, within the bound.
No kernel may reach another device: no remote copies, remote signals or barrier semaphores. Data moves between devices by JAX's collectives and lax.ppermute only.
A program may use at most 128 MiB of HBM per device.

```python
import jax
import jax.numpy as jnp
from jax import lax

HEADS = 16
HEAD_DIM = 128
WINDOW = 512
FIELDS = 64
TOK_DEV = 128
SEQ_LEN = 2048
SEQS = 2


def key_field(key):
    inner_key = jax.random.fold_in(key, 11)
    full_shape = (SEQS, SEQ_LEN, HEADS * HEAD_DIM)
    drawn = jnp.clip(jax.random.normal(inner_key, full_shape, jnp.float32), -6.0, 6.0)
    return drawn


def draw_keys(key, part):
    return key_field(key).astype(jnp.bfloat16)


def draw_queries(key, part):
    inner_key = jax.random.fold_in(key, 12)
    full_shape = (SEQS, SEQ_LEN, HEADS * HEAD_DIM)
    drawn = jnp.clip(jax.random.normal(inner_key, full_shape, jnp.float32), -6.0, 6.0)
    return drawn.astype(jnp.bfloat16)


def draw_lengths(key, part):
    drawn = jax.random.randint(jax.random.fold_in(key, 21), (SEQS,), SEQ_LEN // 8, SEQ_LEN + 1, dtype=jnp.int32)
    chosen = jax.random.randint(jax.random.fold_in(key, 22), (), 0, SEQS, dtype=jnp.int32)
    places = jnp.arange(SEQS, dtype=jnp.int32)
    shortest = jnp.where(places == (chosen + 1) % SEQS, SEQ_LEN // 8, drawn)
    return jnp.where(places == chosen, SEQ_LEN, shortest).astype(jnp.int32)


def plant(entries, stream_key, least, high):
    place = [jax.random.randint(jax.random.fold_in(stream_key, axis), (), 0, length) for axis, length in enumerate(entries.shape)]
    longest = entries.shape.index(max(entries.shape))
    beside = place[:longest] + [(place[longest] + 1) % entries.shape[longest]] + place[longest + 1:]
    return entries.at[tuple(place)].set(least).at[tuple(beside)].set(high)


def levels(own_key, extent, cuts, smallest, high):
    def one(axis_at, parts):
        heights = jax.random.uniform(jax.random.fold_in(jax.random.fold_in(own_key, 6), axis_at), (parts,), jnp.float32, smallest / len(cuts), high / len(cuts))
        return jnp.repeat(jnp.exp(heights), extent[axis_at] // parts).reshape((-1,) + (1,) * (len(extent) - axis_at - 1))

    level = one(*cuts[0])
    for cut in cuts[1:]:
        level = level * one(*cut)
    return level


def scatter_about(rng, shape, scale, most, pieces=(), held_as=jnp.bfloat16):
    entries = jax.random.normal(rng, shape, jnp.float32) * scale
    if len(pieces) > 0:
        entries = levels(rng, shape, pieces, -0.22, 0.18) * entries
    return jnp.clip(entries, min=-most, max=most).astype(held_as)


def setup_inputs(seed: int = 0) -> dict:
    key_list = jax.random.split(jax.random.key(seed), 8)
    return {
        "queries": draw_queries(jax.random.fold_in(key_list[7], 71), 0),
        "keys": draw_keys(jax.random.fold_in(key_list[7], 71), 0),
        "values": scatter_about(key_list[2], (SEQS, SEQ_LEN, HEADS * HEAD_DIM), 1.0, 6.0, ((0, 2), (1, 16))),
        "grad_out": scatter_about(key_list[3], (SEQS, SEQ_LEN, HEADS * HEAD_DIM), 8.0, 48.0, ((0, 2), (1, 16))),
        "lengths": draw_lengths(jax.random.fold_in(key_list[7], 71), 0),
        "fields": plant(jax.random.randint(key_list[5], (SEQS, SEQ_LEN), 0, FIELDS), jax.random.fold_in(key_list[5], 1), 0, FIELDS - 1).astype(jnp.int32),
        "field_bias": scatter_about(key_list[6], (HEADS, FIELDS), 1.0, 6.0),
    }


def head_split(rows):
    return rows.reshape(rows.shape[0], HEADS, HEAD_DIM).astype(jnp.float32)


def band_mask(query_places, key_places, length):
    not_after = key_places[None, :] <= query_places[:, None]
    inside = key_places[None, :] > query_places[:, None] - WINDOW
    started = key_places[None, :] >= 0
    live_rows = query_places[:, None] < length
    return not_after & inside & started & live_rows


def block_grads(query_rows, key_rows, value_rows, grad_rows, key_bias, query_places, key_places, length):
    factor = HEAD_DIM ** -0.5
    query_heads = head_split(query_rows)
    key_heads = head_split(key_rows)
    value_heads = head_split(value_rows)
    grad_heads = head_split(grad_rows)
    logits = jnp.einsum("qhd,khd->hqk", query_heads, key_heads) * factor + key_bias[:, None, :]
    visible = band_mask(query_places, key_places, length)[None]
    row_peak = jnp.max(jnp.where(visible, logits, -1e30), axis=2, keepdims=True)
    powers = jnp.where(visible, jnp.exp(logits - row_peak), 0.0)
    live_rows = (query_places < length)[None, :, None]
    totals = jnp.where(live_rows, jnp.sum(powers, axis=2, keepdims=True), 1.0)
    attn_weights = powers / totals
    weights_low = lax.optimization_barrier(attn_weights.astype(jnp.bfloat16)).astype(jnp.float32)
    outputs = jnp.einsum("hqk,khd->qhd", weights_low, value_heads)
    row_delta = jnp.einsum("qhd,qhd->hq", grad_heads, outputs)
    grad_probs = jnp.einsum("qhd,khd->hqk", grad_heads, value_heads)
    grad_logits = attn_weights * (grad_probs - row_delta[:, :, None])
    grad_low = lax.optimization_barrier(grad_logits.astype(jnp.bfloat16)).astype(jnp.float32)
    grad_query = jnp.einsum("hqk,khd->qhd", grad_low, key_heads) * factor
    grad_key = jnp.einsum("hqk,qhd->khd", grad_low, query_heads) * factor
    grad_value = jnp.einsum("hqk,qhd->khd", weights_low, grad_heads)
    column = jnp.sum(grad_logits, axis=1)
    return grad_query, grad_key, grad_value, column


def reference(queries, keys, values, grad_out, lengths, fields, field_bias):
    bias_table = field_bias.astype(jnp.float32)
    row_width = HEADS * HEAD_DIM
    key_span = WINDOW + TOK_DEV

    def one_sequence(sequence_items):
        query_seq, key_seq, value_seq, grad_seq, length, field_seq = sequence_items
        key_pad = jnp.concatenate([jnp.zeros((WINDOW, row_width), key_seq.dtype), key_seq], axis=0)
        value_pad = jnp.concatenate([jnp.zeros((WINDOW, row_width), value_seq.dtype), value_seq], axis=0)
        field_pad = jnp.concatenate([jnp.full((WINDOW,), -1, jnp.int32), field_seq.astype(jnp.int32)], axis=0)

        def step(carry_state, block_number):
            key_acc, value_acc, bias_acc = carry_state
            first_row = (block_number * TOK_DEV).astype(jnp.int32)
            query_rows = lax.dynamic_slice_in_dim(query_seq, first_row, TOK_DEV, 0)
            grad_rows = lax.dynamic_slice_in_dim(grad_seq, first_row, TOK_DEV, 0)
            key_rows = lax.dynamic_slice_in_dim(key_pad, first_row, key_span, 0)
            value_rows = lax.dynamic_slice_in_dim(value_pad, first_row, key_span, 0)
            field_rows = lax.dynamic_slice_in_dim(field_pad, first_row, key_span, 0)
            onehot = (field_rows[:, None] == jnp.arange(FIELDS, dtype=jnp.int32)[None, :]).astype(jnp.float32)
            key_bias = jnp.dot(bias_table, onehot.T, precision=lax.Precision.HIGHEST)
            query_places = first_row + jnp.arange(TOK_DEV, dtype=jnp.int32)
            key_places = first_row - WINDOW + jnp.arange(key_span, dtype=jnp.int32)
            grad_query, grad_key, grad_value, column = block_grads(
                query_rows, key_rows, value_rows, grad_rows, key_bias, query_places, key_places, length)
            old_keys = lax.dynamic_slice_in_dim(key_acc, first_row, key_span, 0)
            key_acc = lax.dynamic_update_slice_in_dim(key_acc, old_keys + grad_key.reshape(key_span, row_width), first_row, 0)
            old_values = lax.dynamic_slice_in_dim(value_acc, first_row, key_span, 0)
            value_acc = lax.dynamic_update_slice_in_dim(value_acc, old_values + grad_value.reshape(key_span, row_width), first_row, 0)
            bias_acc = bias_acc + jnp.dot(column, onehot, precision=lax.Precision.HIGHEST)
            return (key_acc, value_acc, bias_acc), grad_query.reshape(TOK_DEV, row_width).astype(jnp.bfloat16)

        initial = (jnp.zeros((SEQ_LEN + WINDOW, row_width), jnp.float32),
                   jnp.zeros((SEQ_LEN + WINDOW, row_width), jnp.float32),
                   jnp.zeros((HEADS, FIELDS), jnp.float32))
        final_state, query_blocks = lax.scan(step, initial, jnp.arange(SEQ_LEN // TOK_DEV, dtype=jnp.int32))
        key_acc, value_acc, bias_acc = final_state
        return (query_blocks.reshape(SEQ_LEN, row_width), key_acc[WINDOW:].astype(jnp.bfloat16),
                value_acc[WINDOW:].astype(jnp.bfloat16), bias_acc)

    grad_queries, grad_keys, grad_values, bias_parts = lax.map(
        one_sequence, (queries, keys, values, grad_out, lengths, fields))
    return grad_queries, grad_keys, grad_values, jnp.sum(bias_parts, axis=0)
```

```python
import functools

import jax
import jax.numpy as jnp
from jax import lax
from jax.experimental import pallas as pl
from jax.experimental.pallas import tpu as pltpu
from jax.sharding import PartitionSpec as P

HEADS = 16
HEAD_DIM = 128
WINDOW = 512
FIELDS = 64
FACTOR = HEAD_DIM ** (-0.5)
LOG2E = 1.4426950408889634
HIDDEN = -1e30
PAD = 16
CHUNKS = 2
MIB = 1 << 20
BF16, F32 = jnp.bfloat16, jnp.float32
ANY = pl.BlockSpec(memory_space=pl.ANY)
SMEM = pl.BlockSpec(memory_space=pltpu.SMEM)
NT = (((1,), (1,)), ((), ()))


def dot(a, b):
    return jnp.dot(a, b, preferred_element_type=F32)


def dot_nt(a, b):
    return lax.dot_general(a, b, NT, preferred_element_type=F32)


def run_copies(copies):
    for copy in copies:
        copy.start()
    for copy in copies:
        copy.wait()


def fields_row(fields_ref, width):
    row = fields_ref[...].astype(F32)
    row = jnp.concatenate([row] * (width // row.shape[1]), axis=1)
    return jnp.broadcast_to(row, (PAD, width)).astype(BF16)


def pack_kernel(reach, tok, width, chunk, meta, q, g, k, v, fields, *rest):
    outs, field_scr, sems = rest[: reach - 1], rest[-2], rest[-1]
    p = meta[0]
    field_scr[...] = fields_row(fields, width)
    copies = []
    for m in range(1, reach):
        first = pl.multiple_of((p ^ m) * (HEADS // reach * HEAD_DIM) + chunk * width, 128)
        pairs = [
            (src.at[0, :, pl.ds(first, width)], outs[m - 1].at[pl.ds(at * tok, tok)])
            for at, src in enumerate((q, g, k, v))
        ]
        pairs.append((field_scr, outs[m - 1].at[pl.ds(4 * tok, PAD)]))
        for src, dst in pairs:
            copies.append(pltpu.make_async_copy(src, dst, sems.at[len(copies)]))
    run_copies(copies)


def gather_kernel(reach, tok, width, chunk, meta, q, g, k, v, fields, *rest):
    arrived = rest[: reach - 1]
    qd, kv, field_scr, sems = rest[reach - 1 :]
    p = meta[0]
    field_scr[...] = fields_row(fields, width)
    first = pl.multiple_of(p * (HEADS // reach * HEAD_DIM) + chunk * width, 128)
    own = pl.ds(first, width)
    pairs = [
        (q.at[0, :, own], qd.at[0, pl.ds(0, tok)]),
        (g.at[0, :, own], qd.at[0, pl.ds(tok, tok)]),
        (k.at[0, :, own], kv.at[0, pl.ds(0, tok)]),
        (v.at[0, :, own], kv.at[0, pl.ds(tok, tok)]),
        (field_scr, kv.at[0, pl.ds(2 * tok, PAD)]),
    ]
    for m in range(1, reach):
        pairs.append((arrived[m - 1].at[pl.ds(0, 2 * tok)], qd.at[m]))
        pairs.append((arrived[m - 1].at[pl.ds(2 * tok, 2 * tok + PAD)], kv.at[m]))
    run_copies([pltpu.make_async_copy(s, d, sems.at[i]) for i, (s, d) in enumerate(pairs)])


def unpack_kernel(reach, tok, width, meta, *rest):
    parts, outs, sems = rest[: CHUNKS * reach * 2], rest[CHUNKS * reach * 2 : -1], rest[-1]
    p = meta[0]
    copies = []
    for chunk in range(CHUNKS):
        for m in range(reach):
            dq, dkv = parts[(chunk * reach + m) * 2 : (chunk * reach + m) * 2 + 2]
            first = pl.multiple_of((p ^ m) * (HEADS // reach * HEAD_DIM) + chunk * width, 128)
            there = pl.ds(first, width)
            for src, out in (
                (dq, outs[0]),
                (dkv.at[pl.ds(0, tok)], outs[1]),
                (dkv.at[pl.ds(tok, tok)], outs[2]),
            ):
                copies.append(pltpu.make_async_copy(src, out.at[0, :, there], sems.at[len(copies)]))
    run_copies(copies)


def key_columns(kv, slot, tok):
    row = kv[slot, 2 * tok : 2 * tok + PAD, :].astype(F32)[0:1]
    spread = jnp.broadcast_to(row, (tok, tok))
    lane = lax.broadcasted_iota(jnp.int32, (tok, tok), 1).astype(F32)
    sub = lax.broadcasted_iota(jnp.int32, (tok, tok), 0).astype(F32)
    onehot = jnp.where(spread.T == lane, 1.0, 0.0).astype(BF16)
    onehot_t = jnp.where(spread == sub, 1.0, 0.0).astype(BF16)
    return onehot, onehot_t


def three_parts(x):
    high = x.astype(BF16)
    rest = x - high.astype(F32)
    mid = rest.astype(BF16)
    return high, mid, (rest - mid.astype(F32)).astype(BF16)


def rows_kernel(reach, tok, meta, qd, kvo, kvp, bias_ref, *rest):
    dq_outs = rest[:reach]
    dk_out, dv_out, stats_out, gb_out = rest[reach : reach + 4]
    k_scr, v_scr, kt_scr, oh_scr, oht_scr, bias_scr, acc_scr, dq_scr = rest[reach + 4 :]
    p, plane, length = meta[0], meta[1], meta[2]
    span = reach * tok

    @pl.when(pl.program_id(0) == 0)
    def _():
        for blk in range(2 * reach):
            rows = slice(blk * tok, (blk + 1) * tok)
            onehot, onehot_t = key_columns(kvp if blk < reach else kvo, p ^ (blk % reach), tok)
            oh_scr[rows] = onehot
            oht_scr[:, rows] = onehot_t

    shut = jnp.where(plane == 0, HIDDEN, 0.0).astype(F32)
    for blk in range(2 * reach):
        rows = slice(blk * tok, (blk + 1) * tok)
        src, slot = (kvp if blk < reach else kvo), p ^ (blk % reach)
        key = src[slot, 0:tok, :]
        k_scr[rows] = key
        kt_scr[:, rows] = key.T
        v_scr[rows] = src[slot, tok : 2 * tok, :]
        col = dot(oh_scr[rows], bias_ref[0]) * LOG2E
        bias_scr[rows] = col + shut if blk < reach else col
    acc_scr[...] = jnp.zeros_like(acc_scr)
    key_at = lax.broadcasted_iota(jnp.int32, (tok, tok), 0)
    query_at = lax.broadcasted_iota(jnp.int32, (tok, tok), 1)
    lane = lax.broadcasted_iota(jnp.int32, (1, tok), 1)
    for a in range(reach):
        slot = p ^ a
        query, grad = qd[slot, 0:tok, :], qd[slot, tok : 2 * tok, :]
        rows = slice(a * tok, (a + reach + 1) * tok)
        s = dot_nt(k_scr[rows], query) * (FACTOR * LOG2E) + bias_scr[rows]
        s = jnp.concatenate(
            [
                jnp.where(key_at > query_at, s[:tok], HIDDEN),
                s[tok:-tok],
                jnp.where(key_at <= query_at, s[-tok:], HIDDEN),
            ],
            axis=0,
        )
        peak = jnp.max(s, axis=0, keepdims=True)
        power = jnp.exp2(s - peak)
        total = jnp.sum(power, axis=0, keepdims=True)
        live = plane * span + a * tok + lane < length
        weight = power * jnp.where(live, 1.0 / total, 0.0)
        low = weight.astype(BF16)
        probs = dot_nt(v_scr[rows], grad)
        delta = jnp.sum(low.astype(F32) * probs, axis=0, keepdims=True)
        ds = weight * (probs - delta)
        ds_low = ds.astype(BF16)
        acc_scr[rows] += ds
        dq_scr[slot] = (dot(kt_scr[:, rows], ds_low).T * FACTOR).astype(BF16)
        own = slice((reach - a) * tok, (reach + 1) * tok)
        dv = dot(low[own], grad)
        dk = dot(ds_low[own], query)
        if a:
            dv_out[0 : a * tok] += dv[: a * tok]
            dk_out[0 : a * tok] += dk[: a * tok]
        dv_out[a * tok : (a + 1) * tok] = dv[a * tok :]
        dk_out[a * tok : (a + 1) * tok] = dk[a * tok :]
        there = slice(a * tok, (a + 1) * tok)
        stats_out[0, 0:1, there] = peak + jnp.log2(total)
        stats_out[0, 1:2, there] = delta
    for m in range(reach):
        dq_outs[m][...] = dq_scr[m]
    by_field = sum(dot(oht_scr[...], part) for part in three_parts(acc_scr[...]))
    gb_out[0] = jnp.sum(by_field.T.reshape(tok // 8, 8, tok), axis=0)


def columns_kernel(reach, tok, meta, qd, kvo, stats, bias_ref, dk_in, dv_in, *rest):
    outs = rest[:reach]
    k_scr, v_scr, bias_scr, dk_scr, dv_scr, out_scr = rest[reach:]
    p, plane, length = meta[0], meta[1], meta[2]
    span = reach * tok
    for blk in range(reach):
        rows = slice(blk * tok, (blk + 1) * tok)
        slot = p ^ blk
        k_scr[rows] = kvo[slot, 0:tok, :]
        v_scr[rows] = kvo[slot, tok : 2 * tok, :]
        onehot, _ = key_columns(kvo, slot, tok)
        bias_scr[rows] = dot(onehot, bias_ref[0]) * LOG2E
    dk_scr[...] = dk_in[...]
    dv_scr[...] = dv_in[...]
    key_at = lax.broadcasted_iota(jnp.int32, (tok, tok), 0)
    query_at = lax.broadcasted_iota(jnp.int32, (tok, tok), 1)
    lane = lax.broadcasted_iota(jnp.int32, (1, tok), 1)
    for a in range(reach):
        slot = p ^ a
        query, grad = qd[slot, 0:tok, :], qd[slot, tok : 2 * tok, :]
        rows = slice(a * tok, span)
        there = slice(a * tok, (a + 1) * tok)
        live = (plane + 1) * span + a * tok + lane < length
        norm = jnp.where(live, stats[0, 0:1, there], -HIDDEN)
        delta = stats[0, 1:2, there]
        s = dot_nt(k_scr[rows], query) * (FACTOR * LOG2E) + bias_scr[rows]
        weight = jnp.exp2(s - norm)
        first = jnp.where(key_at > query_at, weight[:tok], 0.0)
        weight = jnp.concatenate([first, weight[tok:]], axis=0) if a < reach - 1 else first
        ds = weight * (dot_nt(v_scr[rows], grad) - delta)
        dv_scr[rows] += dot(weight.astype(BF16), grad)
        dk_scr[rows] += dot(ds.astype(BF16), query)
    for blk in range(reach):
        rows = slice(blk * tok, (blk + 1) * tok)
        out_scr[p ^ blk, 0:tok] = (dk_scr[rows] * FACTOR).astype(BF16)
        out_scr[p ^ blk, tok : 2 * tok] = dv_scr[rows].astype(BF16)
    for m in range(reach):
        outs[m][...] = out_scr[m]


def params(*semantics):
    return pltpu.CompilerParams(
        vmem_limit_bytes=40 * MIB, dimension_semantics=semantics if semantics else None
    )


def cost(flops, nbytes, trans=0):
    return pl.CostEstimate(flops=flops, bytes_accessed=nbytes, transcendentals=trans)


def swapped(value, axis, mask):
    count = lax.axis_size(axis)
    return lax.ppermute(value, axis, [(source, source ^ mask) for source in range(count)])


def passed_along(value, axis, steps):
    count = lax.axis_size(axis)
    first, last = max(0, -steps), min(count, count - steps)
    return lax.ppermute(value, axis, [(source, source + steps) for source in range(first, last)])


def shards(queries, keys, values, grad_out, lengths, fields, field_bias):
    tok = queries.shape[1]
    row_width = queries.shape[2]
    reach = WINDOW // tok
    group = HEADS // reach
    per = group // CHUNKS
    width = per * HEAD_DIM
    span = reach * tok
    index = lax.axis_index("seq")
    p = lax.rem(index, reach)
    meta = jnp.stack([p, lax.div(index, reach), lengths[0]]).astype(jnp.int32)
    raw = (queries, grad_out, keys, values)

    def sds(shape, dtype=BF16):
        return jax.ShapeDtypeStruct(shape, dtype)

    vmem = pl.BlockSpec(memory_space=pltpu.VMEM)

    def pack(chunk):
        return pl.pallas_call(
            functools.partial(pack_kernel, reach, tok, width, chunk),
            in_specs=[SMEM] + [ANY] * 4 + [vmem],
            out_specs=[ANY] * (reach - 1),
            out_shape=[sds((4 * tok + PAD, width))] * (reach - 1),
            scratch_shapes=[
                pltpu.VMEM((PAD, width), BF16),
                pltpu.SemaphoreType.DMA((5 * (reach - 1),)),
            ],
            compiler_params=params(),
            name="pack",
        )(meta, *raw, fields)

    def gather(chunk, arrived):
        return pl.pallas_call(
            functools.partial(gather_kernel, reach, tok, width, chunk),
            in_specs=[SMEM] + [ANY] * 4 + [vmem] + [ANY] * (reach - 1),
            out_specs=[ANY] * 2,
            out_shape=[sds((reach, 2 * tok, width)), sds((reach, 2 * tok + PAD, width))],
            scratch_shapes=[
                pltpu.VMEM((PAD, width), BF16),
                pltpu.SemaphoreType.DMA((5 + 2 * (reach - 1),)),
            ],
            compiler_params=params(),
            name="gather",
        )(meta, *raw, fields, *arrived)

    qd_spec = pl.BlockSpec((reach, 2 * tok, HEAD_DIM), lambda h: (0, 0, h))
    kv_spec = pl.BlockSpec((reach, 2 * tok + PAD, HEAD_DIM), lambda h: (0, 0, h))
    bias_spec = pl.BlockSpec((1, tok, HEAD_DIM), lambda h: (h, 0, 0))
    stats_spec = pl.BlockSpec((1, 8, span), lambda h: (h, 0, 0))
    part_spec = pl.BlockSpec((span, HEAD_DIM), lambda h: (0, h))

    def rows_of(qd, kvo, kvp, bias):
        return pl.pallas_call(
            functools.partial(rows_kernel, reach, tok),
            grid=(per,),
            in_specs=[SMEM, qd_spec, kv_spec, kv_spec, bias_spec],
            out_specs=[pl.BlockSpec((tok, HEAD_DIM), lambda h: (0, h))] * reach
            + [part_spec, part_spec, stats_spec, pl.BlockSpec((1, 8, tok), lambda h: (h, 0, 0))],
            out_shape=[sds((tok, width))] * reach
            + [
                sds((span, width), F32),
                sds((span, width), F32),
                sds((per, 8, span), F32),
                sds((per, 8, tok), F32),
            ],
            scratch_shapes=[
                pltpu.VMEM((2 * span, HEAD_DIM), BF16),
                pltpu.VMEM((2 * span, HEAD_DIM), BF16),
                pltpu.VMEM((HEAD_DIM, 2 * span), BF16),
                pltpu.VMEM((2 * span, tok), BF16),
                pltpu.VMEM((tok, 2 * span), BF16),
                pltpu.VMEM((2 * span, tok), F32),
                pltpu.VMEM((2 * span, tok), F32),
                pltpu.VMEM((reach, tok, HEAD_DIM), BF16),
            ],
            compiler_params=params("arbitrary"),
            cost_estimate=cost(per * 12 * span * (span + tok) * HEAD_DIM, 4 * MIB, per * span * span),
            name="rows",
        )(meta, qd, kvo, kvp, bias)

    def columns_of(qd, kvo, stats, bias, dk, dv):
        return pl.pallas_call(
            functools.partial(columns_kernel, reach, tok),
            grid=(per,),
            in_specs=[SMEM, qd_spec, kv_spec, stats_spec, bias_spec, part_spec, part_spec],
            out_specs=[pl.BlockSpec((2 * tok, HEAD_DIM), lambda h: (0, h))] * reach,
            out_shape=[sds((2 * tok, width))] * reach,
            scratch_shapes=[
                pltpu.VMEM((span, HEAD_DIM), BF16),
                pltpu.VMEM((span, HEAD_DIM), BF16),
                pltpu.VMEM((span, tok), F32),
                pltpu.VMEM((span, HEAD_DIM), F32),
                pltpu.VMEM((span, HEAD_DIM), F32),
                pltpu.VMEM((reach, 2 * tok, HEAD_DIM), BF16),
            ],
            compiler_params=params("arbitrary"),
            cost_estimate=cost(per * 4 * span * (span + tok) * HEAD_DIM, 4 * MIB, per * span * span // 2),
            name="columns",
        )(meta, qd, kvo, stats, bias, dk, dv)

    padded = jnp.pad(field_bias, ((0, 0), (0, tok - FIELDS)))
    my_bias = lax.dynamic_slice_in_dim(padded, p * group, group, 0)
    my_bias = jnp.broadcast_to(my_bias[:, :, None], (group, tok, HEAD_DIM))

    packed = [pack(c) for c in range(CHUNKS)]
    arrived = [[swapped(packed[c][m - 1], "seq", m) for m in range(1, reach)] for c in range(CHUNKS)]
    planes = [gather(c, arrived[c]) for c in range(CHUNKS)]
    before = [passed_along(kv, "seq", reach) for _, kv in planes]
    after = [passed_along(qd, "seq", -reach) for qd, _ in planes]
    parts, bias_parts, pending = [], [], []
    for c in range(CHUNKS):
        qd, kv = planes[c]
        bias = my_bias[c * per : (c + 1) * per]
        *dq, dk, dv, stats, gb = rows_of(qd, kv, before[c], bias)
        bias_parts.append(jnp.sum(gb, axis=1)[:, :FIELDS])
        dq = [dq[0]] + [swapped(dq[m], "seq", m) for m in range(1, reach)]
        pending.append((dq, dk, dv, passed_along(stats, "seq", -reach), bias))
    for c in range(CHUNKS):
        dq, dk, dv, stats, bias = pending[c]
        dkv = columns_of(after[c], planes[c][1], stats, bias, dk, dv)
        dkv = [dkv[0]] + [swapped(dkv[m], "seq", m) for m in range(1, reach)]
        for m in range(reach):
            parts += [dq[m], dkv[m]]

    total = jnp.concatenate(bias_parts, axis=0)
    mask = reach
    while mask < lax.axis_size("seq"):
        total = total + swapped(total, "seq", mask)
        mask *= 2
    mask = 1
    while mask < lax.axis_size("dp"):
        total = total + swapped(total, "dp", mask)
        mask *= 2
    mask = 1
    while mask < reach:
        other = swapped(total, "seq", mask)
        total = jnp.where(
            p & mask > 0,
            jnp.concatenate([other, total], axis=0),
            jnp.concatenate([total, other], axis=0),
        )
        mask *= 2

    grads = pl.pallas_call(
        functools.partial(unpack_kernel, reach, tok, width),
        in_specs=[SMEM] + [ANY] * len(parts),
        out_specs=[ANY] * 3,
        out_shape=[sds((1, tok, row_width))] * 3,
        scratch_shapes=[pltpu.SemaphoreType.DMA((CHUNKS * reach * 3,))],
        compiler_params=params(),
        name="unpack",
    )(meta, *parts)
    return (*grads, total)


def solution(mesh):
    return jax.shard_map(
        shards,
        mesh=mesh,
        in_specs=(
            P("dp", "seq", None),
            P("dp", "seq", None),
            P("dp", "seq", None),
            P("dp", "seq", None),
            P("dp"),
            P("dp", "seq"),
            P(),
        ),
        out_specs=(P("dp", "seq", None), P("dp", "seq", None), P("dp", "seq", None), P()),
        check_vma=False,
    )
```

```python
import functools

import jax
import jax.numpy as jnp
from jax import lax
from jax.experimental import pallas as pl
from jax.experimental.pallas import tpu as pltpu
from jax.sharding import PartitionSpec as P

HEADS = 16
HEAD_DIM = 128
WINDOW = 512
FIELDS = 64
FACTOR = HEAD_DIM ** (-0.5)
LOG2E = 1.4426950408889634
HIDDEN = -1e30
PAD = 16
CHUNKS = 2
MIB = 1 << 20
BF16, F32 = jnp.bfloat16, jnp.float32
ANY = pl.BlockSpec(memory_space=pl.ANY)
SMEM = pl.BlockSpec(memory_space=pltpu.SMEM)
NT = (((1,), (1,)), ((), ()))


def dot(a, b):
    return jnp.dot(a, b, preferred_element_type=F32)


def dot_nt(a, b):
    return lax.dot_general(a, b, NT, preferred_element_type=F32)


def run_copies(copies):
    for copy in copies:
        copy.start()
    for copy in copies:
        copy.wait()


def fields_row(fields_ref, width):
    row = fields_ref[...].astype(F32)
    row = jnp.concatenate([row] * (width // row.shape[1]), axis=1)
    return jnp.broadcast_to(row, (PAD, width)).astype(BF16)


def pack_kernel(reach, tok, width, chunk, meta, q, g, k, v, fields, *rest):
    outs, field_scr, sems = rest[:reach], rest[-2], rest[-1]
    p = meta[0]
    half = outs[0].shape[0] // 2
    field_scr[...] = fields_row(fields, width)
    copies = []
    for m in range(reach):
        first = pl.multiple_of((p ^ m) * (HEADS // reach * HEAD_DIM) + chunk * width, 128)
        pairs = [
            (src.at[0, :, pl.ds(first, width)], outs[m].at[pl.ds(at, tok)])
            for src, at in ((q, 0), (g, tok), (k, half), (v, half + tok))
        ]
        if half > 2 * tok:
            pairs += [(field_scr, outs[m].at[pl.ds(at + 2 * tok, PAD)]) for at in (0, half)]
        for src, dst in pairs:
            copies.append(pltpu.make_async_copy(src, dst, sems.at[len(copies)]))
    run_copies(copies)


def gather_kernel(reach, *refs):
    arrived, outs, sems = refs[:reach], refs[reach:-1], refs[-1]
    half = arrived[0].shape[0] // 2
    copies = []
    for m in range(reach):
        for at, out in enumerate(outs):
            src = arrived[m].at[pl.ds(at * half, half)]
            copies.append(pltpu.make_async_copy(src, out.at[m], sems.at[len(copies)]))
    run_copies(copies)


def unpack_kernel(reach, tok, meta, *rest):
    parts, outs, stage, sems = rest[:reach], rest[reach:-2], rest[-2], rest[-1]
    p = meta[0]
    width = stage.shape[1]
    staging = pltpu.make_async_copy(parts[0], stage, sems.at[3 * reach])
    staging.start()
    copies = []
    for m in list(range(1, reach)) + [0]:
        part = parts[m] if m else stage
        first = pl.multiple_of((p ^ m) * width, 128)
        if m == 0:
            staging.wait()
        for at, out in enumerate(outs):
            src, dst = part.at[pl.ds(at * tok, tok)], out.at[0, :, pl.ds(first, width)]
            copies.append(pltpu.make_async_copy(src, dst, sems.at[len(copies)]))
            copies[-1].start()
    for copy in copies:
        copy.wait()


def key_columns(fields, slot, tok):
    row = fields[slot].astype(F32)[0:1]
    spread = jnp.broadcast_to(row, (tok, tok))
    lane = lax.broadcasted_iota(jnp.int32, (tok, tok), 1).astype(F32)
    sub = lax.broadcasted_iota(jnp.int32, (tok, tok), 0).astype(F32)
    onehot = jnp.where(spread.T == lane, 1.0, 0.0).astype(BF16)
    onehot_t = jnp.where(spread == sub, 1.0, 0.0).astype(BF16)
    return onehot, onehot_t


def three_parts(x):
    high = x.astype(BF16)
    rest = x - high.astype(F32)
    mid = rest.astype(BF16)
    return high, mid, (rest - mid.astype(F32)).astype(BF16)


def masks(tok):
    key_at = lax.broadcasted_iota(jnp.int32, (tok, tok), 0)
    query_at = lax.broadcasted_iota(jnp.int32, (tok, tok), 1)
    return key_at > query_at, lax.broadcasted_iota(jnp.int32, (1, tok), 1)


def query_pair(qd, p, a, tok):
    slots = (p ^ a, p ^ (a + 1))
    query = jnp.concatenate([qd[slot, 0:tok, :] for slot in slots], axis=0)
    grad = jnp.concatenate([qd[slot, tok : 2 * tok, :] for slot in slots], axis=0)
    return query, grad


def side_by_side(first, second, tok, ends):
    gap = jnp.zeros((tok, tok), first.dtype)
    first = jnp.concatenate([first, gap], axis=0) if ends else first
    return jnp.concatenate([first, jnp.concatenate([gap, second], axis=0)], axis=1)


def rows_kernel(reach, tok, meta, qd, kvo, kvp, fo, fp, bias_ref, dq_out, dk_out, dv_out, stats_out, gb_out, *scratch):
    k_scr, v_scr, kt_scr, oh_scr, oht_scr, bias_scr, acc_scr = scratch
    p, plane, length = meta[0], meta[1], meta[2]
    span = reach * tok

    @pl.when(pl.program_id(0) == 0)
    def _():
        for blk in range(2 * reach):
            rows = slice(blk * tok, (blk + 1) * tok)
            onehot, onehot_t = key_columns(fp if blk < reach else fo, p ^ (blk % reach), tok)
            oh_scr[rows] = onehot
            oht_scr[:, rows] = onehot_t

    shut = jnp.where(plane == 0, HIDDEN, 0.0).astype(F32)
    for blk in range(2 * reach):
        rows = slice(blk * tok, (blk + 1) * tok)
        src, slot = (kvp if blk < reach else kvo), p ^ (blk % reach)
        key = src[slot, 0:tok, :]
        k_scr[rows] = key
        kt_scr[:, rows] = key.T
        v_scr[rows] = src[slot, tok : 2 * tok, :]
        col = dot(oh_scr[rows], bias_ref[0]) * LOG2E
        bias_scr[rows] = col + shut if blk < reach else col
    acc_scr[...] = jnp.zeros_like(acc_scr)
    later, lane = masks(tok)
    for pair in range(0, reach, 2):
        query, grad = query_pair(qd, p, pair, tok)
        wide = slice(pair * tok, (pair + reach + 2) * tok)
        logits = dot_nt(k_scr[wide], query)
        probs_both = dot_nt(v_scr[wide], grad)
        lows, ds_lows = [], []
        for half in range(2):
            a = pair + half
            rows = slice(a * tok, (a + reach + 1) * tok)
            mine = slice(half * tok, (half + reach + 1) * tok)
            there = slice(a * tok, (a + 1) * tok)
            cols = slice(half * tok, (half + 1) * tok)
            s = logits[mine, cols] * (FACTOR * LOG2E) + bias_scr[rows]
            s = jnp.concatenate(
                [jnp.where(later, s[:tok], HIDDEN), s[tok:-tok], jnp.where(later, HIDDEN, s[-tok:])],
                axis=0,
            )
            peak = jnp.max(s, axis=0, keepdims=True)
            power = jnp.exp2(s - peak)
            total = jnp.sum(power, axis=0, keepdims=True)
            live = plane * span + a * tok + lane < length
            weight = power * jnp.where(live, 1.0 / total, 0.0)
            low = weight.astype(BF16)
            probs = probs_both[mine, cols]
            delta = jnp.sum(low.astype(F32) * probs, axis=0, keepdims=True)
            ds = weight * (probs - delta)
            acc_scr[rows] += ds
            lows.append(low)
            ds_lows.append(ds.astype(BF16))
            stats_out[0, 0:1, there] = peak + jnp.log2(total)
            stats_out[0, 1:2, there] = delta
        low = side_by_side(*lows, tok, True)
        ds_low = side_by_side(*ds_lows, tok, True)
        dq = dot(kt_scr[:, wide], ds_low)
        for half in range(2):
            dq_half = dq[:, half * tok : (half + 1) * tok]
            dq_out[p ^ (pair + half)] = (dq_half.T * FACTOR).astype(BF16)
        own = slice((reach - pair) * tok, (reach + 2) * tok)
        dv = dot(low[own], grad)
        dk = dot(ds_low[own], query)
        done = pair * tok
        if pair:
            dv_out[0:done] += dv[:done]
            dk_out[0:done] += dk[:done]
        dv_out[done : done + 2 * tok] = dv[done:]
        dk_out[done : done + 2 * tok] = dk[done:]
    by_field = sum(dot(oht_scr[...], part) for part in three_parts(acc_scr[...]))
    gb_out[0] = jnp.sum(by_field.T.reshape(tok // 8, 8, tok), axis=0)


def columns_kernel(reach, tok, meta, qd, kvo, fo, stats, bias_ref, dq_in, dk_in, dv_in, *rest):
    outs = rest[-6 - reach : -6]
    k_scr, v_scr, bias_scr, dk_scr, dv_scr, out_scr = rest[-6:]
    p, plane, length = meta[0], meta[1], meta[2]
    span = reach * tok
    for blk in range(reach):
        rows = slice(blk * tok, (blk + 1) * tok)
        slot = p ^ blk
        k_scr[rows] = kvo[slot, 0:tok, :]
        v_scr[rows] = kvo[slot, tok : 2 * tok, :]
        onehot, _ = key_columns(fo, slot, tok)
        bias_scr[rows] = dot(onehot, bias_ref[0]) * LOG2E
    later, lane = masks(tok)
    for pair in range(0, reach, 2):
        query, grad = query_pair(qd, p, pair, tok)
        wide = slice(pair * tok, span)
        logits = dot_nt(k_scr[wide], query)
        probs_both = dot_nt(v_scr[wide], grad)
        lows, ds_lows = [], []
        for half in range(2):
            a = pair + half
            there = slice(a * tok, (a + 1) * tok)
            cols = slice(half * tok, (half + 1) * tok)
            live = (plane + 1) * span + a * tok + lane < length
            norm = jnp.where(live, stats[0, 0:1, there], -HIDDEN)
            delta = stats[0, 1:2, there]
            s = logits[half * tok :, cols] * (FACTOR * LOG2E) + bias_scr[a * tok :]
            weight = jnp.exp2(s - norm)
            first = jnp.where(later, weight[:tok], 0.0)
            weight = jnp.concatenate([first, weight[tok:]], axis=0) if a < reach - 1 else first
            lows.append(weight.astype(BF16))
            ds_lows.append((weight * (probs_both[half * tok :, cols] - delta)).astype(BF16))
        dv = dot(side_by_side(*lows, tok, False), grad)
        dk = dot(side_by_side(*ds_lows, tok, False), query)
        dv_scr[wide] = dv + (dv_scr if pair else dv_in)[wide]
        dk_scr[wide] = dk + (dk_scr if pair else dk_in)[wide]
    for blk in range(reach):
        rows = slice(blk * tok, (blk + 1) * tok)
        out_scr[p ^ blk, 0:tok] = (dk_scr[rows] * FACTOR).astype(BF16)
        out_scr[p ^ blk, tok : 2 * tok] = dv_scr[rows].astype(BF16)
    for m in range(reach):
        outs[m][0:tok] = dq_in[m]
        outs[m][tok : 3 * tok] = out_scr[m]


def params(mib, *semantics):
    return pltpu.CompilerParams(
        vmem_limit_bytes=mib * MIB, dimension_semantics=semantics if semantics else None
    )


def cost(flops, nbytes, trans=0):
    return pl.CostEstimate(flops=flops, bytes_accessed=nbytes, transcendentals=trans)


def in_hbm(*arrays):
    return [pltpu.with_memory_space_constraint(array, pltpu.HBM) for array in arrays]


def in_vmem(*arrays):
    return [pltpu.with_memory_space_constraint(array, pltpu.VMEM) for array in arrays]


def following(value, mark):
    return lax.optimization_barrier((value, mark))[0]


def swapped(value, axis, mask):
    count = lax.axis_size(axis)
    return lax.ppermute(value, axis, [(source, source ^ mask) for source in range(count)])


def passed_along(value, axis, steps):
    count = lax.axis_size(axis)
    first, last = max(0, -steps), min(count, count - steps)
    return lax.ppermute(value, axis, [(source, source + steps) for source in range(first, last)])


def shards(queries, keys, values, grad_out, lengths, fields, field_bias):
    tok = queries.shape[1]
    row_width = queries.shape[2]
    reach = WINDOW // tok
    group = HEADS // reach
    per = group // CHUNKS
    width = per * HEAD_DIM
    span = reach * tok
    index = lax.axis_index("seq")
    p = lax.rem(index, reach)
    meta = jnp.stack([p, lax.div(index, reach), lengths[0]]).astype(jnp.int32)
    raw = in_hbm(queries, grad_out, keys, values)

    def hbm(shape, dtype=BF16):
        return pltpu.HBM(shape, dtype)

    vmem = pl.BlockSpec(memory_space=pltpu.VMEM)

    def rows_in(chunk):
        return 2 * tok + (PAD if chunk == 0 else 0)

    def pack(chunk):
        return pl.pallas_call(
            functools.partial(pack_kernel, reach, tok, width, chunk),
            in_specs=[SMEM] + [ANY] * 4 + [vmem],
            out_specs=[ANY] * reach,
            out_shape=[pltpu.VMEM((2 * rows_in(chunk), width), BF16)] * reach,
            scratch_shapes=[
                pltpu.VMEM((PAD, width), BF16),
                pltpu.SemaphoreType.DMA((6 * reach,)),
            ],
            compiler_params=params(2),
            cost_estimate=cost(0, 2 * MIB),
            name="pack",
        )(meta, *raw, fields)

    def gather(chunk, arrived):
        return pl.pallas_call(
            functools.partial(gather_kernel, reach),
            in_specs=[ANY] * reach,
            out_specs=[ANY] * 2,
            out_shape=[hbm((reach, rows_in(chunk), width))] * 2,
            scratch_shapes=[pltpu.SemaphoreType.DMA((2 * reach,))],
            compiler_params=params(2),
            cost_estimate=cost(2 * 10**9 if chunk else 0, 2 * MIB),
            name="gather",
        )(*in_vmem(*arrived))

    qd_spec = pl.BlockSpec((reach, 2 * tok, HEAD_DIM), lambda h: (0, 0, h))
    fields_spec = pl.BlockSpec((reach, PAD, HEAD_DIM), lambda h: (0, 2 * tok // PAD, 0))
    bias_spec = pl.BlockSpec((1, tok, HEAD_DIM), lambda h: (h, 0, 0))
    stats_spec = pl.BlockSpec((1, 8, span), lambda h: (h, 0, 0))
    part_spec = pl.BlockSpec((span, HEAD_DIM), lambda h: (0, h))

    dq_spec = pl.BlockSpec((reach, tok, HEAD_DIM), lambda h: (0, 0, h))

    def rows_of(qd, kvo, kvp, fo, fp, bias):
        return pl.pallas_call(
            functools.partial(rows_kernel, reach, tok),
            grid=(per,),
            in_specs=[SMEM, qd_spec, qd_spec, qd_spec, fields_spec, fields_spec, bias_spec],
            out_specs=[dq_spec, part_spec, part_spec, stats_spec, pl.BlockSpec((1, 8, tok), lambda h: (h, 0, 0))],
            out_shape=[
                hbm((reach, tok, width)),
                hbm((span, width), F32),
                hbm((span, width), F32),
                hbm((per, 8, span), F32),
                jax.ShapeDtypeStruct((per, 8, tok), F32),
            ],
            scratch_shapes=[
                pltpu.VMEM((2 * span, HEAD_DIM), BF16),
                pltpu.VMEM((2 * span, HEAD_DIM), BF16),
                pltpu.VMEM((HEAD_DIM, 2 * span), BF16),
                pltpu.VMEM((2 * span, tok), BF16),
                pltpu.VMEM((tok, 2 * span), BF16),
                pltpu.VMEM((2 * span, tok), F32),
                pltpu.VMEM((2 * span, tok), F32),
            ],
            compiler_params=params(20, "arbitrary"),
            cost_estimate=cost(per * 56 * span * (span + tok) * HEAD_DIM * 1, 4 * MIB),
            name="rows",
        )(meta, *in_hbm(qd, kvo), kvp, *in_hbm(fo), fp, bias)

    def columns_of(chunk, qd, kvo, fo, stats, bias, dq, dk, dv, *messages):
        return pl.pallas_call(
            functools.partial(columns_kernel, reach, tok),
            grid=(per,),
            in_specs=[SMEM, qd_spec, qd_spec, fields_spec, stats_spec, bias_spec, dq_spec, part_spec, part_spec]
            + [ANY] * len(messages),
            out_specs=[pl.BlockSpec((3 * tok, HEAD_DIM), lambda h: (0, chunk * per + h))] * reach,
            out_shape=[hbm((3 * tok, group * HEAD_DIM))] * reach,
            input_output_aliases={9 + m: m for m in range(len(messages))},
            scratch_shapes=[
                pltpu.VMEM((span, HEAD_DIM), BF16),
                pltpu.VMEM((span, HEAD_DIM), BF16),
                pltpu.VMEM((span, tok), F32),
                pltpu.VMEM((span, HEAD_DIM), F32),
                pltpu.VMEM((span, HEAD_DIM), F32),
                pltpu.VMEM((reach, 2 * tok, HEAD_DIM), BF16),
            ],
            compiler_params=params(20, "arbitrary"),
            cost_estimate=cost(per * 28 * span * (span + tok) * HEAD_DIM * 1, 4 * MIB),
            name="columns",
        )(meta, qd, *in_hbm(kvo, fo), stats, bias, *in_hbm(dq, dk, dv, *messages))

    padded = jnp.pad(field_bias, ((0, 0), (0, tok - FIELDS)))
    my_bias = lax.dynamic_slice_in_dim(padded, p * group, group, 0)
    my_bias = jnp.broadcast_to(my_bias[:, :, None], (group, tok, HEAD_DIM))

    packed = [list(pack(c)) for c in range(CHUNKS)]
    packed[0][0] = following(packed[0][0], packed[1][0])
    planes, before, after = [], [], []
    for c in range(CHUNKS):
        arrived = packed[c][:1] + [swapped(packed[c][m], "seq", m) for m in range(1, reach)]
        qd, kv = gather(c, arrived)
        planes.append((qd, kv))
        moved = passed_along(kv, "seq", reach), passed_along(qd, "seq", -reach)
        before.append(following(moved[0], moved[1]) if c == 0 else moved[0])
        after.append(moved[1])
    bias_parts, pending = [], []
    for c in range(CHUNKS):
        bias = my_bias[c * per : (c + 1) * per]
        dq, dk, dv, stats, gb = rows_of(*planes[c], before[c], planes[0][1], before[0], bias)
        bias_parts.append(jnp.sum(gb, axis=1)[:, :FIELDS])
        pending.append((passed_along(stats, "seq", -reach), bias, dq, dk, dv))
    messages = []
    for c in range(CHUNKS):
        messages = columns_of(c, after[c], planes[c][1], planes[0][1], *pending[c], *messages)
    parts = [messages[0]] + [swapped(messages[m], "seq", m) for m in range(1, reach)]

    total = jnp.concatenate(bias_parts, axis=0)
    total = following(total, messages[0])
    mask = reach
    while mask < lax.axis_size("seq"):
        total = total + swapped(total, "seq", mask)
        mask *= 2
    mask = 1
    while mask < lax.axis_size("dp"):
        total = total + swapped(total, "dp", mask)
        mask *= 2
    mask = 1
    while mask < reach:
        other = swapped(total, "seq", mask)
        total = jnp.where(
            p & mask > 0,
            jnp.concatenate([other, total], axis=0),
            jnp.concatenate([total, other], axis=0),
        )
        mask *= 2

    grads = pl.pallas_call(
        functools.partial(unpack_kernel, reach, tok),
        in_specs=[SMEM] + [ANY] * reach,
        out_specs=[ANY] * 3,
        out_shape=[jax.ShapeDtypeStruct((1, tok, row_width), BF16)] * 3,
        scratch_shapes=[
            pltpu.VMEM((3 * tok, group * HEAD_DIM), BF16),
            pltpu.SemaphoreType.DMA((3 * reach + 1,)),
        ],
        compiler_params=params(4),
        name="unpack",
    )(meta, *in_hbm(parts[0]), *in_vmem(*parts[1:]))
    return (*grads, total)


def solution(mesh):
    return jax.shard_map(
        shards,
        mesh=mesh,
        in_specs=(
            P("dp", "seq", None),
            P("dp", "seq", None),
            P("dp", "seq", None),
            P("dp", "seq", None),
            P("dp"),
            P("dp", "seq"),
            P(),
        ),
        out_specs=(P("dp", "seq", None), P("dp", "seq", None), P("dp", "seq", None), P()),
        check_vma=False,
    )
```

```python
import functools

import jax
import jax.numpy as jnp
from jax import lax
from jax.experimental import pallas as pl
from jax.experimental.pallas import tpu as pltpu
from jax.sharding import PartitionSpec as P

HEADS = 16
HEAD_DIM = 128
WINDOW = 512
FIELDS = 64
FACTOR = HEAD_DIM ** (-0.5)
LOG2E = 1.4426950408889634
HIDDEN = -1e30
PAD = 16
CHUNKS = 2
MIB = 1 << 20
BF16, F32 = jnp.bfloat16, jnp.float32
ANY = pl.BlockSpec(memory_space=pl.ANY)
SMEM = pl.BlockSpec(memory_space=pltpu.SMEM)
VMEM = pl.BlockSpec(memory_space=pltpu.VMEM)
GATHER_FLOPS, ROWS_FLOPS, COLUMNS_FLOPS, UNPACK_FLOPS = 2 * 10**9, 2 * 10**9, (4 * 10**9, 0), 0
NT = (((1,), (1,)), ((), ()))


def dot(a, b):
    return jnp.dot(a, b, preferred_element_type=F32)


def dot_nt(a, b):
    return lax.dot_general(a, b, NT, preferred_element_type=F32)


def pack_kernel(reach, tok, width, chunk, meta, q, g, k, v, fields, *rest):
    outs, field_scr, sems = rest[:reach], rest[-2], rest[-1]
    p = meta[0]
    field_copy = pltpu.make_async_copy(fields, field_scr, sems.at[4 * reach])
    field_copy.start()
    copies = []
    for m in list(range(1, reach)) + [0]:
        first = pl.multiple_of((p ^ m) * (HEADS // reach * HEAD_DIM) + chunk * width, 128)
        for at, src in enumerate((q, g, k, v)):
            dst = outs[m].at[pl.ds(at * tok, tok)]
            copies.append(pltpu.make_async_copy(src.at[0, :, pl.ds(first, width)], dst, sems.at[len(copies)]))
            copies[-1].start()
    field_copy.wait()
    row = jnp.concatenate([field_scr[...].astype(F32)] * (width // tok), axis=1)
    for out in outs:
        if out.shape[0] > 4 * tok:
            out[4 * tok :] = jnp.broadcast_to(row, (PAD, width)).astype(BF16)
    for copy in copies:
        copy.wait()


def gather_kernel(reach, tok, *refs):
    arrived, qd, kv = refs[:reach], *refs[reach:]
    for m in range(reach):
        qd[m] = arrived[m][: 2 * tok]
        kv[m] = arrived[m][2 * tok :]


def unpack_kernel(reach, tok, group_width, blocks, meta, *rest):
    parts, outs, sems = rest[:reach], rest[-4:-1], rest[-1]
    p = meta[0]
    width = parts[0].shape[1]
    copies = []
    for m in range(reach):
        for at, (which, chunk) in enumerate(blocks):
            first = pl.multiple_of((p ^ m) * group_width + chunk * width, 128)
            dst = outs[which].at[0, :, pl.ds(first, width)]
            copies.append(pltpu.make_async_copy(parts[m].at[pl.ds(at * tok, tok)], dst, sems.at[len(copies)]))
            copies[-1].start()
    for copy in copies:
        copy.wait()


def finish_kernel(reach, tok, group_width, blocks, meta, *rest):
    total, sems = rest[-2:]
    join(reach, tok, len(blocks) * tok, meta[0], rest[:reach], total)
    unpack_kernel(reach, tok, group_width, blocks, meta, *rest[:-2], sems)


def key_columns(fields, slot, tok):
    row = fields[slot, 2 * tok : 2 * tok + PAD, 0:tok].astype(F32)[0:1]
    spread = jnp.broadcast_to(row, (tok, tok))
    lane = lax.broadcasted_iota(jnp.int32, (tok, tok), 1).astype(F32)
    sub = lax.broadcasted_iota(jnp.int32, (tok, tok), 0).astype(F32)
    onehot = jnp.where(spread.T == lane, 1.0, 0.0).astype(BF16)
    onehot_t = jnp.where(spread == sub, 1.0, 0.0).astype(BF16)
    return onehot, onehot_t


def head_bias(bias_ref, head, tok):
    table = bias_ref[...].astype(F32)
    at = lax.broadcasted_iota(jnp.int32, table.shape, 0)
    row = jnp.sum(jnp.where(at == head, table, 0.0), axis=0, keepdims=True)
    row = jnp.concatenate([row, jnp.zeros((1, tok - FIELDS), F32)], axis=1)
    return jnp.broadcast_to(row, (tok, tok)).T.astype(BF16)


def three_parts(x):
    high = x.astype(BF16)
    rest = x - high.astype(F32)
    mid = rest.astype(BF16)
    return high, mid, (rest - mid.astype(F32)).astype(BF16)


def masks(tok):
    key_at = lax.broadcasted_iota(jnp.int32, (tok, tok), 0)
    query_at = lax.broadcasted_iota(jnp.int32, (tok, tok), 1)
    return key_at > query_at, lax.broadcasted_iota(jnp.int32, (1, tok), 1)


def query_pair(qd, p, a, tok, head):
    slots = (p ^ a, p ^ (a + 1))
    query = jnp.concatenate([qd[slot, 0:tok, head] for slot in slots], axis=0)
    grad = jnp.concatenate([qd[slot, tok : 2 * tok, head] for slot in slots], axis=0)
    return query, grad


def side_by_side(first, second, tok, ends):
    gap = jnp.zeros((tok, tok), first.dtype)
    first = jnp.concatenate([first, gap], axis=0) if ends else first
    return jnp.concatenate([first, jnp.concatenate([gap, second], axis=0)], axis=1)


def rows_kernel(reach, tok, chunk, meta, qd, kvo, kvp, fo, fp, bias_ref, sums_in, *rest):
    dq_out, dk_out, dv_out, stats_out, sums_out, *scratch = rest
    k_scr, v_scr, kt_scr, oh_scr, oht_scr, bias_scr, acc_scr = scratch
    p, plane, length = meta[0], meta[1], meta[2]
    span = reach * tok

    for blk in range(2 * reach):
        rows = slice(blk * tok, (blk + 1) * tok)
        onehot, onehot_t = key_columns(fp if blk < reach else fo, p ^ (blk % reach), tok)
        oh_scr[rows] = onehot
        oht_scr[:, rows] = onehot_t
    per = kvo.shape[2] // HEAD_DIM
    sums_out[...] = sums_in[...]
    shut = jnp.where(plane == 0, HIDDEN, 0.0).astype(F32)
    later, lane = masks(tok)

    @pl.loop(0, kvo.shape[2] // HEAD_DIM)
    def _(h):
        head = pl.ds(pl.multiple_of(h * HEAD_DIM, HEAD_DIM), HEAD_DIM)
        at = chunk * per + h
        bias = head_bias(bias_ref, p * (HEADS // reach) + at, tok)
        for blk in range(2 * reach):
            rows = slice(blk * tok, (blk + 1) * tok)
            src, slot = (kvp if blk < reach else kvo), p ^ (blk % reach)
            key = src[slot, 0:tok, head]
            k_scr[rows] = key
            kt_scr[:, rows] = key.T
            v_scr[rows] = src[slot, tok : 2 * tok, head]
            col = dot(oh_scr[rows], bias) * LOG2E
            bias_scr[rows] = col + shut if blk < reach else col
        acc_scr[...] = jnp.zeros_like(acc_scr)
        for pair in range(0, reach, 2):
            query, grad = query_pair(qd, p, pair, tok, head)
            wide = slice(pair * tok, (pair + reach + 2) * tok)
            logits = dot_nt(k_scr[wide], query)
            probs_both = dot_nt(v_scr[wide], grad)
            lows, ds_lows = [], []
            for half in range(2):
                a = pair + half
                rows = slice(a * tok, (a + reach + 1) * tok)
                mine = slice(half * tok, (half + reach + 1) * tok)
                there = slice(a * tok, (a + 1) * tok)
                cols = slice(half * tok, (half + 1) * tok)
                s = logits[mine, cols] * (FACTOR * LOG2E) + bias_scr[rows]
                s = jnp.concatenate(
                    [jnp.where(later, s[:tok], HIDDEN), s[tok:-tok], jnp.where(later, HIDDEN, s[-tok:])],
                    axis=0,
                )
                peak = jnp.max(s, axis=0, keepdims=True)
                power = jnp.exp2(s - peak)
                total = jnp.sum(power, axis=0, keepdims=True)
                live = plane * span + a * tok + lane < length
                weight = power * jnp.where(live, 1.0 / total, 0.0)
                low = weight.astype(BF16)
                probs = probs_both[mine, cols]
                delta = jnp.sum(low.astype(F32) * probs, axis=0, keepdims=True)
                ds = weight * (probs - delta)
                acc_scr[rows] += ds
                lows.append(low)
                ds_lows.append(ds.astype(BF16))
                stats_out[h, 0:1, there] = peak + jnp.log2(total)
                stats_out[h, 1:2, there] = delta
            low = side_by_side(*lows, tok, True)
            ds_low = side_by_side(*ds_lows, tok, True)
            dq = dot(kt_scr[:, wide], ds_low)
            for half in range(2):
                dq_half = dq[:, half * tok : (half + 1) * tok]
                dq_out[p ^ (pair + half), :, head] = (dq_half.T * FACTOR).astype(BF16)
            own = slice((reach - pair) * tok, (reach + 2) * tok)
            dv = dot(low[own], grad)
            dk = dot(ds_low[own], query)
            done = pair * tok
            if pair:
                dv_out[0:done, head] += dv[:done]
                dk_out[0:done, head] += dk[:done]
            dv_out[done : done + 2 * tok, head] = dv[done:]
            dk_out[done : done + 2 * tok, head] = dk[done:]
        by_field = sum(dot(oht_scr[...], part) for part in three_parts(acc_scr[...]))
        row = jnp.sum(by_field.T, axis=0, keepdims=True)
        sums_out[...] += jnp.where(lax.broadcasted_iota(jnp.int32, (8, tok), 0) == at, row, 0.0)


def columns_kernel(reach, tok, chunk, meta, qd, kvo, fo, stats, bias_ref, dk_in, dv_in, *rest):
    k_scr, v_scr, oh_scr, bias_scr, dk_scr, dv_scr = rest[-6:]
    outs, extras = rest[-6 - reach : -6], rest[: -6 - reach]
    last = len(extras) == 1
    if last:
        parts = [part.astype(F32) for part in three_parts(extras[0][...])]
        parts = [jnp.concatenate(parts[:2], axis=1), jnp.concatenate([parts[2], jnp.zeros_like(parts[2])], axis=1)]
        for m in range(reach):
            outs[m][2 * tok :] = jnp.concatenate(parts, axis=0).astype(BF16)
    p, plane, length = meta[0], meta[1], meta[2]
    span = reach * tok
    for blk in range(reach):
        oh_scr[blk * tok : (blk + 1) * tok], _ = key_columns(fo, p ^ blk, tok)
    later, lane = masks(tok)

    @pl.loop(0, kvo.shape[2] // HEAD_DIM)
    def _(h):
        head = pl.ds(pl.multiple_of(h * HEAD_DIM, HEAD_DIM), HEAD_DIM)
        at = chunk * (kvo.shape[2] // HEAD_DIM) + h
        bias = head_bias(bias_ref, p * (HEADS // reach) + at, tok)
        for blk in range(reach):
            rows = slice(blk * tok, (blk + 1) * tok)
            k_scr[rows] = kvo[p ^ blk, 0:tok, head]
            v_scr[rows] = kvo[p ^ blk, tok : 2 * tok, head]
            bias_scr[rows] = dot(oh_scr[rows], bias) * LOG2E
        for pair in range(0, reach, 2):
            query, grad = query_pair(qd, p, pair, tok, head)
            wide = slice(pair * tok, span)
            logits = dot_nt(k_scr[wide], query)
            probs_both = dot_nt(v_scr[wide], grad)
            lows, ds_lows = [], []
            for half in range(2):
                a = pair + half
                there = slice(a * tok, (a + 1) * tok)
                cols = slice(half * tok, (half + 1) * tok)
                live = (plane + 1) * span + a * tok + lane < length
                norm = jnp.where(live, stats[h, 0:1, there], -HIDDEN)
                delta = stats[h, 1:2, there]
                s = logits[half * tok :, cols] * (FACTOR * LOG2E) + bias_scr[a * tok :]
                weight = jnp.exp2(s - norm)
                first = jnp.where(later, weight[:tok], 0.0)
                weight = jnp.concatenate([first, weight[tok:]], axis=0) if a < reach - 1 else first
                lows.append(weight.astype(BF16))
                ds_lows.append((weight * (probs_both[half * tok :, cols] - delta)).astype(BF16))
            dv = dot(side_by_side(*lows, tok, False), grad)
            dk = dot(side_by_side(*ds_lows, tok, False), query)
            if pair:
                dv_scr[wide] += dv
                dk_scr[wide] += dk
            else:
                dv_scr[...] = dv + dv_in[:, head]
                dk_scr[...] = dk + dk_in[:, head]
        for m in range(reach):
            mine = pl.ds(pl.multiple_of((p ^ m) * tok, tok), tok)
            outs[m][0:tok, head] = (dk_scr[mine] * FACTOR).astype(BF16)
            outs[m][tok : 2 * tok, head] = dv_scr[mine].astype(BF16)
            for at, dq in enumerate(() if last else extras):
                outs[m][(2 + at) * tok : (3 + at) * tok, head] = dq[m, :, head]


def add_kernel(reach, tok, a, b, out):
    out[...] = a[...] + b[...]


def join(reach, tok, first, p, slots, out):
    heads = HEADS // reach
    found = []
    for slot in slots:
        rows = slot[first : first + PAD].astype(F32)
        found.append(rows[:8, :FIELDS] + rows[:8, tok : tok + FIELDS] + rows[8:, :FIELDS])
    for q in range(reach):
        part = found[0]
        for m in range(1, reach):
            part = jnp.where(p == q ^ m, found[m], part)
        out[q * heads : (q + 1) * heads] = part[:heads]


def params(mib, *semantics):
    return pltpu.CompilerParams(
        vmem_limit_bytes=mib * MIB, dimension_semantics=semantics if semantics else None
    )


def cost(flops, nbytes, trans=0):
    return pl.CostEstimate(flops=flops, bytes_accessed=nbytes, transcendentals=trans)


def in_hbm(*arrays):
    return [pltpu.with_memory_space_constraint(array, pltpu.HBM) for array in arrays]


def in_vmem(*arrays):
    return [pltpu.with_memory_space_constraint(array, pltpu.VMEM) for array in arrays]


def following(value, mark):
    return lax.optimization_barrier((value, mark))[0]


def swapped(value, axis, mask):
    count = lax.axis_size(axis)
    return lax.ppermute(value, axis, [(source, source ^ mask) for source in range(count)])


def passed_along(value, axis, steps):
    count = lax.axis_size(axis)
    first, last = max(0, -steps), min(count, count - steps)
    return lax.ppermute(value, axis, [(source, source + steps) for source in range(first, last)])


def shards(queries, keys, values, grad_out, lengths, fields, field_bias):
    tok = queries.shape[1]
    row_width = queries.shape[2]
    reach = WINDOW // tok
    group = HEADS // reach
    per = group // CHUNKS
    width = per * HEAD_DIM
    span = reach * tok
    index = lax.axis_index("seq")
    p = lax.rem(index, reach)
    meta = jnp.stack([p, lax.div(index, reach), lengths[0]]).astype(jnp.int32)
    raw = in_hbm(queries, grad_out, keys, values)

    def vmem(shape, dtype=BF16):
        return pltpu.VMEM(shape, dtype)


    def pad(chunk):
        return 0 if chunk else PAD

    def pack(chunk):
        return pl.pallas_call(
            functools.partial(pack_kernel, reach, tok, width, chunk),
            in_specs=[SMEM] + [ANY] * 5,
            out_specs=[VMEM] * reach,
            out_shape=[pltpu.VMEM((4 * tok + pad(chunk), width), BF16)] * reach,
            scratch_shapes=[
                pltpu.VMEM((1, tok), jnp.int32),
                pltpu.SemaphoreType.DMA((4 * reach + 1,)),
            ],
            compiler_params=params(2),
            cost_estimate=cost(0, 2 * MIB),
            name="pack",
        )(meta, *raw, *in_hbm(fields))

    def local(kernel, name, flops, out_shape, *args, scratch=()):
        return pl.pallas_call(
            kernel,
            in_specs=[SMEM if arg is meta else VMEM for arg in args],
            out_specs=[VMEM] * len(out_shape),
            out_shape=out_shape,
            scratch_shapes=scratch,
            compiler_params=params(12),
            cost_estimate=cost(flops, 2 * MIB),
            name=name,
        )(*[arg if arg is meta else in_vmem(arg)[0] for arg in args])

    def gather(chunk, arrived):
        out = [vmem((reach, 2 * tok, width)), vmem((reach, 2 * tok + pad(chunk), width))]
        return local(functools.partial(gather_kernel, reach, tok), "gather", GATHER_FLOPS if chunk else 0, out, *arrived)

    def rows_of(chunk, qd, kvo, kvp, fo, fp, sums):
        out = [
            vmem((reach, tok, width)),
            vmem((span, width), F32),
            vmem((span, width), F32),
            vmem((per, 2, span), F32),
            vmem((8, tok), F32),
        ]
        scratch = [
            pltpu.VMEM((2 * span, HEAD_DIM), BF16),
            pltpu.VMEM((2 * span, HEAD_DIM), BF16),
            pltpu.VMEM((HEAD_DIM, 2 * span), BF16),
            pltpu.VMEM((2 * span, tok), BF16),
            pltpu.VMEM((tok, 2 * span), BF16),
            pltpu.VMEM((2 * span, tok), F32),
            pltpu.VMEM((2 * span, tok), F32),
        ]
        kernel = functools.partial(rows_kernel, reach, tok, chunk)
        return local(kernel, "rows", ROWS_FLOPS, out, meta, qd, kvo, kvp, fo, fp, field_bias, sums, scratch=scratch)

    def columns_of(chunk, qd, kvo, fo, stats, dk, dv, *extras):
        out = [vmem((2 * tok + (PAD if len(extras) == 1 else len(extras) * tok), width))] * reach
        scratch = [
            pltpu.VMEM((span, HEAD_DIM), BF16),
            pltpu.VMEM((span, HEAD_DIM), BF16),
            pltpu.VMEM((span, tok), BF16),
            pltpu.VMEM((span, tok), F32),
            pltpu.VMEM((span, HEAD_DIM), F32),
            pltpu.VMEM((span, HEAD_DIM), F32),
        ]
        kernel = functools.partial(columns_kernel, reach, tok, chunk)
        args = (meta, qd, kvo, fo, stats, field_bias, dk, dv, *extras)
        return local(kernel, "columns", COLUMNS_FLOPS[chunk], out, *args, scratch=scratch)

    def add(a, b):
        return local(functools.partial(add_kernel, reach, tok), "add", 0, [vmem(a.shape, F32)], a, b)[0]

    packed = [list(pack(c)) for c in range(CHUNKS)]
    packed[0][0] = following(packed[0][0], packed[1][0])
    planes, before, after = [], [], []
    for c in range(CHUNKS):
        arrived = packed[c][:1] + [swapped(packed[c][m], "seq", m) for m in range(1, reach)]
        qd, kv = gather(c, arrived)
        planes.append((qd, kv))
        moved = passed_along(kv, "seq", reach), passed_along(qd, "seq", -reach)
        before.append(following(moved[0], moved[1]) if c == 0 else moved[0])
        after.append(moved[1])
    sums = jnp.zeros((8, tok), F32)
    pending, dqs = [], []
    for c in range(CHUNKS):
        dq, dk, dv, stats, sums = rows_of(c, *planes[c], before[c], planes[0][1], before[0], sums)
        dqs.append(dq)
        pending.append((after[c], planes[c][1], planes[0][1], passed_along(following(stats, after[c]), "seq", -reach), dk, dv))
    messages = [columns_of(0, *pending[0], *dqs)]
    count = lax.axis_size("seq")
    mask = reach
    while mask < count:
        sums = add(sums, swapped(sums, "seq", mask))
        if mask == reach:
            messages[0] = [following(following(own, sums), pending[1][3]) for own in messages[0]]
        mask *= 2
    mask = 1
    while mask < lax.axis_size("dp"):
        sums = add(sums, swapped(sums, "dp", mask))
        mask *= 2
    messages.append(columns_of(1, *pending[1], sums))
    parts = [[own[0]] + [swapped(own[m], "seq", m) for m in range(1, reach)] for own in messages]

    blocks = [((1, 0), (2, 0), (0, 0), (0, 1)), ((1, 1), (2, 1))]
    grads = []
    for c in range(CHUNKS):
        last = c == CHUNKS - 1
        kernel = finish_kernel if last else unpack_kernel
        out = [jax.ShapeDtypeStruct((1, tok, row_width), BF16)] * 3
        grads = pl.pallas_call(
            functools.partial(kernel, reach, tok, group * HEAD_DIM, blocks[c]),
            in_specs=[SMEM] + [VMEM] * reach + [ANY] * len(grads),
            out_specs=[ANY] * 3 + [VMEM] * last,
            out_shape=out + [jax.ShapeDtypeStruct((HEADS, FIELDS), F32)] * last,
            scratch_shapes=[pltpu.SemaphoreType.DMA((len(blocks[c]) * reach,))],
            input_output_aliases={1 + reach + at: at for at in range(len(grads))},
            compiler_params=params(2),
            cost_estimate=cost(0 if last else UNPACK_FLOPS, 2 * MIB),
            name="unpack",
        )(meta, *in_vmem(*parts[c]), *grads)
    return grads


def solution(mesh):
    return jax.shard_map(
        shards,
        mesh=mesh,
        in_specs=(
            P("dp", "seq", None),
            P("dp", "seq", None),
            P("dp", "seq", None),
            P("dp", "seq", None),
            P("dp"),
            P("dp", "seq"),
            P(),
        ),
        out_specs=(P("dp", "seq", None), P("dp", "seq", None), P("dp", "seq", None), P()),
        check_vma=False,
    )
```

```python
import functools

import jax
import jax.numpy as jnp
from jax import lax
from jax.experimental import pallas as pl
from jax.experimental.pallas import tpu as pltpu
from jax.sharding import PartitionSpec as P

HEADS = 16
HEAD_DIM = 128
WINDOW = 512
FIELDS = 64
FACTOR = HEAD_DIM ** (-0.5)
LOG2E = 1.4426950408889634
HIDDEN = -1e30
PAD = 16
CHUNKS = 2
MIB = 1 << 20
BF16, F32 = jnp.bfloat16, jnp.float32
ANY = pl.BlockSpec(memory_space=pl.ANY)
VMEM = pl.BlockSpec(memory_space=pltpu.VMEM)
GATHER_FLOPS, ROWS_FLOPS, COLUMNS_FLOPS, PAIR_FLOPS = 2 * 10**9, 2 * 10**9, (4 * 10**9, 0), 8 * 10**9
NT = (((1,), (1,)), ((), ()))


def dot(a, b):
    return jnp.dot(a, b, preferred_element_type=F32)


def dot_nt(a, b):
    return lax.dot_general(a, b, NT, preferred_element_type=F32)


def place(reach):
    index = lax.axis_index("seq")
    return lax.rem(index, reach), lax.div(index, reach)


def pack_kernel(reach, tok, width, chunk, q, g, k, v, fields, *rest):
    outs, field_scr, sems = rest[:reach], rest[-2], rest[-1]
    p, _ = place(reach)
    field_copy = pltpu.make_async_copy(fields, field_scr, sems.at[4 * reach])
    field_copy.start()
    copies = []
    for m in list(range(1, reach)) + [0]:
        first = pl.multiple_of((p ^ m) * (HEADS // reach * HEAD_DIM) + chunk * width, 128)
        for at, src in enumerate((q, g, k, v)):
            dst = outs[m].at[pl.ds(at * tok, tok)]
            copies.append(pltpu.make_async_copy(src.at[0, :, pl.ds(first, width)], dst, sems.at[len(copies)]))
            copies[-1].start()
    field_copy.wait()
    row = jnp.concatenate([field_scr[...].astype(F32)] * (width // tok), axis=1)
    for out in outs:
        if out.shape[0] > 4 * tok:
            out[4 * tok :] = jnp.broadcast_to(row, (PAD, width)).astype(BF16)
    for copy in copies:
        copy.wait()


def gather_kernel(reach, tok, *refs):
    arrived, qd, kv = refs[:reach], *refs[reach:]
    for m in range(reach):
        qd[m] = arrived[m][: 2 * tok]
        kv[m] = arrived[m][2 * tok :]


def unpack_kernel(reach, tok, group_width, blocks, *rest):
    parts, outs, sems = rest[:reach], rest[-4:-1], rest[-1]
    p, _ = place(reach)
    width = parts[0].shape[1]
    copies = []
    for m in range(reach):
        for at, (which, chunk) in enumerate(blocks):
            first = pl.multiple_of((p ^ m) * group_width + chunk * width, 128)
            dst = outs[which].at[0, :, pl.ds(first, width)]
            copies.append(pltpu.make_async_copy(parts[m].at[pl.ds(at * tok, tok)], dst, sems.at[len(copies)]))
            copies[-1].start()
    for copy in copies:
        copy.wait()


def finish_kernel(reach, tok, group_width, blocks, *rest):
    total, sems = rest[-2:]
    join(reach, tok, len(blocks) * tok, place(reach)[0], rest[:reach], total)
    unpack_kernel(reach, tok, group_width, blocks, *rest[:-2], sems)


def onehot_of(fields, slot, tok):
    row = fields[slot, 2 * tok : 2 * tok + PAD, 0:tok].astype(F32)[0:1]
    lane = lax.broadcasted_iota(jnp.int32, (tok, tok), 1)
    lane = jnp.where(lane < FIELDS, lane, lane - FIELDS).astype(F32)
    return jnp.where(jnp.broadcast_to(row, (tok, tok)).T == lane, 1.0, 0.0).astype(BF16)


def bias_rows(bias_ref, head, tok):
    table = bias_ref[...].astype(F32)
    at = lax.broadcasted_iota(jnp.int32, table.shape, 0)
    row = jnp.sum(jnp.where(at == head, table, 0.0), axis=0, keepdims=True) * (1.0 / FACTOR)
    high = row.astype(BF16).astype(F32)
    return jnp.broadcast_to(jnp.concatenate([high, row - high], axis=1), (2 * tok, tok)).astype(BF16)


def three_parts(x):
    high = x.astype(BF16)
    rest = x - high.astype(F32)
    mid = rest.astype(BF16)
    return high, mid, (rest - mid.astype(F32)).astype(BF16)


def masks(tok):
    key_at = lax.broadcasted_iota(jnp.int32, (tok, tok), 0)
    query_at = lax.broadcasted_iota(jnp.int32, (tok, tok), 1)
    return key_at > query_at, lax.broadcasted_iota(jnp.int32, (1, tok), 1)


def query_pair(qd, p, a, tok, head):
    slots = (p ^ a, p ^ (a + 1))
    query = jnp.concatenate([qd[slot, 0:tok, head] for slot in slots], axis=0)
    grad = jnp.concatenate([qd[slot, tok : 2 * tok, head] for slot in slots], axis=0)
    return query, grad


def side_by_side(first, second, tok, ends):
    gap = jnp.zeros((tok, tok), first.dtype)
    first = jnp.concatenate([first, gap], axis=0) if ends else first
    return jnp.concatenate([first, jnp.concatenate([gap, second], axis=0)], axis=1)


def rows_kernel(reach, tok, chunk, lengths, qd, kvo, kvp, bias_ref, sums_in, *rest):
    *onehots, dq_out, dk_out, dv_out, stats_out, sums_out, k_scr, v_scr, kt_scr, acc_scr = rest
    onehots = onehots[0]
    p, plane = place(reach)
    length = lengths[...]
    span = reach * tok

    for blk in range(2 * reach):
        rows = slice(blk * tok, (blk + 1) * tok)
        if chunk == 0:
            onehots[rows] = onehot_of(kvp if blk < reach else kvo, p ^ (blk % reach), tok)
        k_scr[rows, HEAD_DIM:] = onehots[rows]
    per = kvo.shape[2] // HEAD_DIM
    sums_out[...] = sums_in[...]
    shut = jnp.where(plane == 0, HIDDEN, 0.0).astype(F32)
    later, lane = masks(tok)

    @pl.loop(0, kvo.shape[2] // HEAD_DIM, unroll=True)
    def _(h):
        head = pl.ds(pl.multiple_of(h * HEAD_DIM, HEAD_DIM), HEAD_DIM)
        at = chunk * per + h
        bias = bias_rows(bias_ref, p * (HEADS // reach) + at, tok)
        for blk in range(2 * reach):
            rows = slice(blk * tok, (blk + 1) * tok)
            src, slot = (kvp if blk < reach else kvo), p ^ (blk % reach)
            key = src[slot, 0:tok, head]
            k_scr[rows, :HEAD_DIM] = key
            kt_scr[:, rows] = key.T
            v_scr[rows] = src[slot, tok : 2 * tok, head]
        acc_scr[...] = jnp.zeros_like(acc_scr)
        for pair in range(0, reach, 2):
            query, grad = query_pair(qd, p, pair, tok, head)
            wide = slice(pair * tok, (pair + reach + 2) * tok)
            logits = dot_nt(k_scr[wide], jnp.concatenate([query, bias], axis=1))
            probs_both = dot_nt(v_scr[wide], grad)
            lows, ds_lows = [], []
            for half in range(2):
                a = pair + half
                rows = slice(a * tok, (a + reach + 1) * tok)
                mine = slice(half * tok, (half + reach + 1) * tok)
                there = slice(a * tok, (a + 1) * tok)
                cols = slice(half * tok, (half + 1) * tok)
                s = logits[mine, cols] * (FACTOR * LOG2E)
                seen = [jnp.where(later, s[:tok], HIDDEN) + shut, s[tok : (reach - a) * tok] + shut]
                seen += [s[(reach - a) * tok : -tok], jnp.where(later, HIDDEN, s[-tok:])]
                s = jnp.concatenate([part for part in seen if part.shape[0]], axis=0)
                peak = jnp.max(s, axis=0, keepdims=True)
                power = jnp.exp2(s - peak)
                total = jnp.sum(power, axis=0, keepdims=True)
                live = plane * span + a * tok + lane < length
                weight = power * jnp.where(live, 1.0 / total, 0.0)
                low = weight.astype(BF16)
                probs = probs_both[mine, cols]
                delta = jnp.sum(low.astype(F32) * probs, axis=0, keepdims=True)
                ds = weight * (probs - delta)
                acc_scr[rows] += ds
                lows.append(low)
                ds_lows.append(ds.astype(BF16))
                stats_out[h, 0:1, there] = peak + jnp.log2(total)
                stats_out[h, 1:2, there] = delta
            low = side_by_side(*lows, tok, True)
            ds_low = side_by_side(*ds_lows, tok, True)
            dq = dot(kt_scr[:, wide], ds_low)
            for half in range(2):
                dq_half = dq[:, half * tok : (half + 1) * tok]
                dq_out[p ^ (pair + half), :, head] = (dq_half.T * FACTOR).astype(BF16)
            own = slice((reach - pair) * tok, (reach + 2) * tok)
            dv = dot(low[own], grad)
            dk = dot(ds_low[own], query)
            done = pair * tok
            if pair:
                dv_out[0:done, head] += dv[:done]
                dk_out[0:done, head] += dk[:done]
            dv_out[done : done + 2 * tok, head] = dv[done:]
            dk_out[done : done + 2 * tok, head] = dk[done:]
        by_key = jnp.sum(acc_scr[...], axis=1, keepdims=True)
        row = jnp.sum(by_key * onehots[...].astype(F32), axis=0, keepdims=True)
        sums_out[...] += jnp.where(lax.broadcasted_iota(jnp.int32, (8, tok), 0) == at, row, 0.0)

    if stats_out.shape[0] > per:
        for h in range(HEADS // reach):
            stats_out[per, 0:1, h * tok : (h + 1) * tok] = sums_out[h : h + 1]
            stats_out[per, 1:2, h * tok : (h + 1) * tok] = sums_out[h : h + 1]


def pair_kernel(reach, tok, sums, stats, out):
    out[0] = sums[...]
    out[1] = jnp.zeros_like(sums)
    for h in range(HEADS // reach):
        out[1, h : h + 1] = stats[stats.shape[0] - 1, 0:1, h * tok : (h + 1) * tok]


def planes_kernel(reach, tok, *refs):
    _, plane = place(reach)
    parts, out, blocks = refs[:-2], refs[-2], refs[-1]
    count = blocks.shape[0]
    at = 0
    for part in parts:
        blocks[at : at + part.shape[0]] = part[...]
        at += part.shape[0]
    out[...] = blocks[lax.rem(count - plane, count)]
    for q in range(1, count):
        out[...] += blocks[lax.rem(q + count - plane, count)]


def columns_kernel(reach, tok, chunk, lengths, qd, kvo, onehots, stats, bias_ref, dk_in, dv_in, *rest):
    k_scr, v_scr, dk_scr, dv_scr = rest[-4:]
    outs, extras = rest[-4 - reach : -4], rest[: -4 - reach]
    last = len(extras) == 1
    if last:
        parts = [part.astype(F32) for part in three_parts(extras[0][...])]
        parts = [jnp.concatenate(parts[:2], axis=1), jnp.concatenate([parts[2], jnp.zeros_like(parts[2])], axis=1)]
        for m in range(reach):
            outs[m][2 * tok :] = jnp.concatenate(parts, axis=0).astype(BF16)
    p, plane = place(reach)
    length = lengths[...]
    span = reach * tok
    k_scr[:, HEAD_DIM:] = onehots[span:]
    later, lane = masks(tok)

    @pl.loop(0, kvo.shape[2] // HEAD_DIM, unroll=True)
    def _(h):
        head = pl.ds(pl.multiple_of(h * HEAD_DIM, HEAD_DIM), HEAD_DIM)
        at = chunk * (kvo.shape[2] // HEAD_DIM) + h
        bias = bias_rows(bias_ref, p * (HEADS // reach) + at, tok)
        for blk in range(reach):
            rows = slice(blk * tok, (blk + 1) * tok)
            k_scr[rows, :HEAD_DIM] = kvo[p ^ blk, 0:tok, head]
            v_scr[rows] = kvo[p ^ blk, tok : 2 * tok, head]
        for pair in range(0, reach, 2):
            query, grad = query_pair(qd, p, pair, tok, head)
            wide = slice(pair * tok, span)
            logits = dot_nt(k_scr[wide], jnp.concatenate([query, bias], axis=1))
            probs_both = dot_nt(v_scr[wide], grad)
            lows, ds_lows = [], []
            for half in range(2):
                a = pair + half
                there = slice(a * tok, (a + 1) * tok)
                cols = slice(half * tok, (half + 1) * tok)
                live = (plane + 1) * span + a * tok + lane < length
                norm = jnp.where(live, stats[h, 0:1, there], -HIDDEN)
                delta = stats[h, 1:2, there]
                s = logits[half * tok :, cols] * (FACTOR * LOG2E)
                weight = jnp.exp2(s - norm)
                first = jnp.where(later, weight[:tok], 0.0)
                weight = jnp.concatenate([first, weight[tok:]], axis=0) if a < reach - 1 else first
                lows.append(weight.astype(BF16))
                ds_lows.append((weight * (probs_both[half * tok :, cols] - delta)).astype(BF16))
            dv = dot(side_by_side(*lows, tok, False), grad)
            dk = dot(side_by_side(*ds_lows, tok, False), query)
            if pair:
                dv_scr[wide] += dv
                dk_scr[wide] += dk
            else:
                dv_scr[...] = dv + dv_in[:, head]
                dk_scr[...] = dk + dk_in[:, head]
        for m in range(reach):
            mine = pl.ds(pl.multiple_of((p ^ m) * tok, tok), tok)
            outs[m][0:tok, head] = (dk_scr[mine] * FACTOR).astype(BF16)
            outs[m][tok : 2 * tok, head] = dv_scr[mine].astype(BF16)
            for at, dq in enumerate(() if last else extras):
                outs[m][(2 + at) * tok : (3 + at) * tok, head] = dq[m, :, head]


def stack_kernel(*refs):
    parts, out = refs[:-1], refs[-1]
    at = 0
    for part in parts:
        out[at : at + part.shape[0]] = part[...]
        at += part.shape[0]


def add_kernel(reach, tok, a, b, out):
    out[...] = a[...] + b[...]


def join(reach, tok, first, p, slots, out):
    heads = HEADS // reach
    found = []
    for slot in slots:
        rows = slot[first : first + PAD].astype(F32)
        found.append(rows[:8, :FIELDS] + rows[:8, tok : tok + FIELDS] + rows[8:, :FIELDS])
    for q in range(reach):
        part = found[0]
        for m in range(1, reach):
            part = jnp.where(p == q ^ m, found[m], part)
        out[q * heads : (q + 1) * heads] = part[:heads]


def params(mib, *semantics):
    return pltpu.CompilerParams(
        vmem_limit_bytes=mib * MIB, dimension_semantics=semantics if semantics else None
    )


def cost(flops, nbytes, trans=0):
    return pl.CostEstimate(flops=flops, bytes_accessed=nbytes, transcendentals=trans)


def in_hbm(*arrays):
    return [pltpu.with_memory_space_constraint(array, pltpu.HBM) for array in arrays]


def in_vmem(*arrays):
    return [pltpu.with_memory_space_constraint(array, pltpu.VMEM) for array in arrays]


def following(value, mark):
    return lax.optimization_barrier((value, mark))[0]


def swapped(value, axis, mask):
    count = lax.axis_size(axis)
    return lax.ppermute(value, axis, [(source, source ^ mask) for source in range(count)])


def passed_round(value, axis, steps):
    count = lax.axis_size(axis)
    return lax.ppermute(value, axis, [(source, (source + steps) % count) for source in range(count)])


def passed_along(value, axis, steps):
    count = lax.axis_size(axis)
    first, last = max(0, -steps), min(count, count - steps)
    return lax.ppermute(value, axis, [(source, source + steps) for source in range(first, last)])


def shards(queries, keys, values, grad_out, lengths, fields, field_bias):
    tok = queries.shape[1]
    row_width = queries.shape[2]
    reach = WINDOW // tok
    group = HEADS // reach
    per = group // CHUNKS
    width = per * HEAD_DIM
    span = reach * tok
    length = jnp.broadcast_to(lengths[:, None], (1, tok))
    raw = in_hbm(queries, grad_out, keys, values)

    def vmem(shape, dtype=BF16):
        return pltpu.VMEM(shape, dtype)


    def pad(chunk):
        return 0 if chunk else PAD

    def pack(chunk):
        return pl.pallas_call(
            functools.partial(pack_kernel, reach, tok, width, chunk),
            in_specs=[ANY] * 5,
            out_specs=[VMEM] * reach,
            out_shape=[pltpu.VMEM((4 * tok + pad(chunk), width), BF16)] * reach,
            scratch_shapes=[
                pltpu.VMEM((1, tok), jnp.int32),
                pltpu.SemaphoreType.DMA((4 * reach + 1,)),
            ],
            compiler_params=params(2),
            cost_estimate=cost(0, 2 * MIB),
            name="pack",
        )(*raw, *in_hbm(fields))

    def local(kernel, name, flops, out_shape, *args, scratch=()):
        return pl.pallas_call(
            kernel,
            in_specs=[VMEM] * len(args),
            out_specs=[VMEM] * len(out_shape),
            out_shape=out_shape,
            scratch_shapes=scratch,
            compiler_params=params(12),
            cost_estimate=cost(flops, 2 * MIB),
            name=name,
        )(*in_vmem(*args))

    def gather(chunk, arrived):
        out = [vmem((reach, 2 * tok, width)), vmem((reach, 2 * tok + pad(chunk), width))]
        return local(functools.partial(gather_kernel, reach, tok), "gather", GATHER_FLOPS if chunk else 0, out, *arrived)

    def rows_of(chunk, qd, kvo, kvp, sums, *onehots):
        out = [
            vmem((reach, tok, width)),
            vmem((span, width), F32),
            vmem((span, width), F32),
            vmem((per + chunk, 2, span), F32),
            vmem((8, tok), F32),
        ]
        if chunk == 0:
            out = [vmem((2 * span, tok))] + out
        scratch = [
            pltpu.VMEM((2 * span, 2 * HEAD_DIM), BF16),
            pltpu.VMEM((2 * span, HEAD_DIM), BF16),
            pltpu.VMEM((HEAD_DIM, 2 * span), BF16),
            pltpu.VMEM((2 * span, tok), F32),
        ]
        kernel = functools.partial(rows_kernel, reach, tok, chunk)
        args = (length, qd, kvo, kvp, field_bias, sums, *onehots)
        return local(kernel, "rows", ROWS_FLOPS, out, *args, scratch=scratch)

    def columns_of(chunk, qd, kvo, onehots, stats, dk, dv, *extras):
        out = [vmem((2 * tok + (PAD if len(extras) == 1 else len(extras) * tok), width))] * reach
        scratch = [
            pltpu.VMEM((span, 2 * HEAD_DIM), BF16),
            pltpu.VMEM((span, HEAD_DIM), BF16),
            pltpu.VMEM((span, HEAD_DIM), F32),
            pltpu.VMEM((span, HEAD_DIM), F32),
        ]
        kernel = functools.partial(columns_kernel, reach, tok, chunk)
        args = (length, qd, kvo, onehots, stats, field_bias, dk, dv, *extras)
        return local(kernel, "columns", COLUMNS_FLOPS[chunk], out, *args, scratch=scratch)

    def add(a, b):
        return local(functools.partial(add_kernel, reach, tok), "add", 0, [vmem(a.shape, F32)], a, b)[0]

    packed = [list(pack(c)) for c in range(CHUNKS)]
    packed[0][0] = following(packed[0][0], packed[1][0])
    planes, before, after = [], [], []
    for c in range(CHUNKS):
        arrived = packed[c][:1] + [swapped(packed[c][m], "seq", m) for m in range(1, reach)]
        qd, kv = gather(c, arrived)
        planes.append((qd, kv))
        moved = passed_along(kv, "seq", reach), passed_along(qd, "seq", -reach)
        before.append(following(moved[0], moved[1]) if c == 0 else moved[0])
        after.append(moved[1])
    sums = jnp.zeros((8, tok), F32)
    pending, dqs, onehots = [], [], []
    for c in range(CHUNKS):
        *made, dq, dk, dv, stats, sums = rows_of(c, *planes[c], before[c], sums, *onehots)
        onehots = onehots or made
        dqs.append(dq)
        stats = following(stats, after[c])
        stats = passed_round(stats, "seq", -reach) if c else passed_along(stats, "seq", -reach)
        pending.append((after[c], planes[c][1], *onehots, stats, dk, dv))
    messages = [list(columns_of(0, *pending[0], *dqs))]
    messages[0][1] = following(messages[0][1], stats)
    blocks = [local(functools.partial(pair_kernel, reach, tok), "pair", PAIR_FLOPS, [vmem((2, 8, tok), F32)], sums, stats)[0]]
    count = lax.axis_size("seq") // reach
    step = 2
    while step < count:
        so_far = blocks[0]
        if len(blocks) > 1:
            so_far = local(stack_kernel, "stack", 0, [vmem((step, 8, tok), F32)], *blocks)[0]
        blocks.append(passed_round(so_far, "seq", -step * reach))
        step *= 2
    kernel = functools.partial(planes_kernel, reach, tok)
    scratch = [pltpu.VMEM((count, 8, tok), F32)]
    sums = local(kernel, "planes", 0, [vmem((8, tok), F32)], *blocks, scratch=scratch)[0]
    mask = 1
    while mask < lax.axis_size("dp"):
        sums = add(sums, swapped(sums, "dp", mask))
        mask *= 2
    messages.append(columns_of(1, *pending[1], sums))
    parts = [[own[0]] + [swapped(own[m], "seq", m) for m in range(1, reach)] for own in messages]

    blocks = [((1, 0), (2, 0), (0, 0), (0, 1)), ((1, 1), (2, 1))]
    grads = []
    for c in range(CHUNKS):
        last = c == CHUNKS - 1
        kernel = finish_kernel if last else unpack_kernel
        out = [jax.ShapeDtypeStruct((1, tok, row_width), BF16)] * 3
        grads = pl.pallas_call(
            functools.partial(kernel, reach, tok, group * HEAD_DIM, blocks[c]),
            in_specs=[VMEM] * reach + [ANY] * len(grads),
            out_specs=[ANY] * 3 + [VMEM] * last,
            out_shape=out + [jax.ShapeDtypeStruct((HEADS, FIELDS), F32)] * last,
            scratch_shapes=[pltpu.SemaphoreType.DMA((len(blocks[c]) * reach,))],
            input_output_aliases={reach + at: at for at in range(len(grads))},
            compiler_params=params(2),
            cost_estimate=cost(0, 2 * MIB),
            name="unpack",
        )(*in_vmem(*parts[c]), *grads)
    return grads


def solution(mesh):
    return jax.shard_map(
        shards,
        mesh=mesh,
        in_specs=(
            P("dp", "seq", None),
            P("dp", "seq", None),
            P("dp", "seq", None),
            P("dp", "seq", None),
            P("dp"),
            P("dp", "seq"),
            P(),
        ),
        out_specs=(P("dp", "seq", None), P("dp", "seq", None), P("dp", "seq", None), P()),
        check_vma=False,
    )
```

```python
import functools

import jax
import jax.numpy as jnp
from jax import lax
from jax.experimental import pallas as pl
from jax.experimental.pallas import tpu as pltpu
from jax.sharding import PartitionSpec as P

HEADS = 16
HEAD_DIM = 128
WINDOW = 512
FIELDS = 64
FACTOR = HEAD_DIM ** (-0.5)
LOG2E = 1.4426950408889634
HIDDEN = -1e30
PAD = 16
CHUNKS = 2
MIB = 1 << 20
BF16, F32 = jnp.bfloat16, jnp.float32
ANY = pl.BlockSpec(memory_space=pl.ANY)
VMEM = pl.BlockSpec(memory_space=pltpu.VMEM)
GATHER_FLOPS, ROWS_FLOPS, COLUMNS_FLOPS = 2 * 10**9, 2 * 10**9, (4 * 10**9, 0)
NT = (((1,), (1,)), ((), ()))


def dot(a, b):
    return jnp.dot(a, b, preferred_element_type=F32)


def dot_nt(a, b):
    return lax.dot_general(a, b, NT, preferred_element_type=F32)


def place(reach):
    index = lax.axis_index("seq")
    return lax.rem(index, reach), lax.div(index, reach)


def pack_kernel(reach, tok, width, chunk, q, g, k, v, fields, *rest):
    outs, field_scr, sems = rest[:reach], rest[-2], rest[-1]
    p, _ = place(reach)
    field_copy = pltpu.make_async_copy(fields, field_scr, sems.at[4 * reach])
    field_copy.start()
    copies = []
    for m in list(range(1, reach)) + [0]:
        first = pl.multiple_of((p ^ m) * (HEADS // reach * HEAD_DIM) + chunk * width, 128)
        for at, src in enumerate((q, g, k, v)):
            dst = outs[m].at[pl.ds(at * tok, tok)]
            copies.append(pltpu.make_async_copy(src.at[0, :, pl.ds(first, width)], dst, sems.at[len(copies)]))
            copies[-1].start()
    field_copy.wait()
    row = jnp.concatenate([field_scr[...].astype(F32)] * (width // tok), axis=1)
    for out in outs:
        if out.shape[0] > 4 * tok:
            out[4 * tok :] = jnp.broadcast_to(row, (PAD, width)).astype(BF16)
    for copy in copies:
        copy.wait()


def gather_kernel(reach, tok, *refs):
    arrived, qd, kv = refs[:reach], *refs[reach:]
    for m in range(reach):
        qd[m] = arrived[m][: 2 * tok]
        kv[m] = arrived[m][2 * tok :]


def unpack_kernel(reach, tok, group_width, blocks, *rest):
    parts, outs, sems = rest[:reach], rest[-4:-1], rest[-1]
    p, _ = place(reach)
    width = parts[0].shape[1]
    copies = []
    for m in range(reach):
        for at, (which, chunk) in enumerate(blocks):
            first = pl.multiple_of((p ^ m) * group_width + chunk * width, 128)
            dst = outs[which].at[0, :, pl.ds(first, width)]
            copies.append(pltpu.make_async_copy(parts[m].at[pl.ds(at * tok, tok)], dst, sems.at[len(copies)]))
            copies[-1].start()
    for copy in copies:
        copy.wait()


def finish_kernel(reach, tok, group_width, blocks, *rest):
    total, sems = rest[-2:]
    join(reach, tok, len(blocks) * tok, place(reach)[0], rest[:reach], total)
    unpack_kernel(reach, tok, group_width, blocks, *rest[:-2], sems)


def onehot_of(fields, slot, tok):
    row = fields[slot, 2 * tok : 2 * tok + PAD, 0:tok].astype(F32)[0:1]
    lane = lax.broadcasted_iota(jnp.int32, (tok, tok), 1)
    lane = jnp.where(lane < FIELDS, lane, lane - FIELDS).astype(F32)
    return jnp.where(jnp.broadcast_to(row, (tok, tok)).T == lane, 1.0, 0.0).astype(BF16)


def bias_rows(bias_ref, head, tok):
    table = bias_ref[...].astype(F32)
    at = lax.broadcasted_iota(jnp.int32, table.shape, 0)
    row = jnp.sum(jnp.where(at == head, table, 0.0), axis=0, keepdims=True) * (1.0 / FACTOR)
    high = row.astype(BF16).astype(F32)
    return jnp.broadcast_to(jnp.concatenate([high, row - high], axis=1), (2 * tok, tok)).astype(BF16)


def three_parts(x):
    high = x.astype(BF16)
    rest = x - high.astype(F32)
    mid = rest.astype(BF16)
    return high, mid, (rest - mid.astype(F32)).astype(BF16)


def masks(tok):
    key_at = lax.broadcasted_iota(jnp.int32, (tok, tok), 0)
    query_at = lax.broadcasted_iota(jnp.int32, (tok, tok), 1)
    return key_at > query_at, lax.broadcasted_iota(jnp.int32, (1, tok), 1)


def query_pair(qd, p, a, tok, head):
    slots = (p ^ a, p ^ (a + 1))
    query = jnp.concatenate([qd[slot, 0:tok, head] for slot in slots], axis=0)
    grad = jnp.concatenate([qd[slot, tok : 2 * tok, head] for slot in slots], axis=0)
    return query, grad


def side_by_side(first, second, tok, ends):
    gap = jnp.zeros((tok, tok), first.dtype)
    first = jnp.concatenate([first, gap], axis=0) if ends else first
    return jnp.concatenate([first, jnp.concatenate([gap, second], axis=0)], axis=1)


def rows_kernel(reach, tok, chunk, lengths, qd, kvo, kvp, bias_ref, sums_in, *rest):
    *onehots, dq_out, dk_out, dv_out, stats_out, sums_out, k_scr, v_scr, kt_scr, acc_scr = rest
    onehots = onehots[0]
    p, plane = place(reach)
    length = lengths[...]
    span = reach * tok

    for blk in range(2 * reach):
        rows = slice(blk * tok, (blk + 1) * tok)
        if chunk == 0:
            onehots[rows] = onehot_of(kvp if blk < reach else kvo, p ^ (blk % reach), tok)
        k_scr[rows, HEAD_DIM:] = onehots[rows]
    per = kvo.shape[2] // HEAD_DIM
    sums_out[...] = sums_in[...]
    shut = jnp.where(plane == 0, HIDDEN, 0.0).astype(F32)
    later, lane = masks(tok)

    @pl.loop(0, kvo.shape[2] // HEAD_DIM, unroll=True)
    def _(h):
        head = pl.ds(pl.multiple_of(h * HEAD_DIM, HEAD_DIM), HEAD_DIM)
        at = chunk * per + h
        bias = bias_rows(bias_ref, p * (HEADS // reach) + at, tok)
        for blk in range(2 * reach):
            rows = slice(blk * tok, (blk + 1) * tok)
            src, slot = (kvp if blk < reach else kvo), p ^ (blk % reach)
            key = src[slot, 0:tok, head]
            k_scr[rows, :HEAD_DIM] = key
            kt_scr[:, rows] = key.T
            v_scr[rows] = src[slot, tok : 2 * tok, head]
        acc_scr[...] = jnp.zeros_like(acc_scr)
        for pair in range(0, reach, 2):
            query, grad = query_pair(qd, p, pair, tok, head)
            wide = slice(pair * tok, (pair + reach + 2) * tok)
            logits = dot_nt(k_scr[wide], jnp.concatenate([query, bias], axis=1))
            probs_both = dot_nt(v_scr[wide], grad)
            lows, ds_lows = [], []
            for half in range(2):
                a = pair + half
                rows = slice(a * tok, (a + reach + 1) * tok)
                mine = slice(half * tok, (half + reach + 1) * tok)
                there = slice(a * tok, (a + 1) * tok)
                cols = slice(half * tok, (half + 1) * tok)
                s = logits[mine, cols] * (FACTOR * LOG2E)
                seen = [jnp.where(later, s[:tok], HIDDEN) + shut, s[tok : (reach - a) * tok] + shut]
                seen += [s[(reach - a) * tok : -tok], jnp.where(later, HIDDEN, s[-tok:])]
                s = jnp.concatenate([part for part in seen if part.shape[0]], axis=0)
                peak = jnp.max(s, axis=0, keepdims=True)
                power = jnp.exp2(s - peak)
                total = jnp.sum(power, axis=0, keepdims=True)
                live = plane * span + a * tok + lane < length
                weight = power * jnp.where(live, 1.0 / total, 0.0)
                low = weight.astype(BF16)
                probs = probs_both[mine, cols]
                delta = jnp.sum(low.astype(F32) * probs, axis=0, keepdims=True)
                ds = weight * (probs - delta)
                acc_scr[rows] += ds
                lows.append(low)
                ds_lows.append(ds.astype(BF16))
                stats_out[h, 0:1, there] = peak + jnp.log2(total)
                stats_out[h, 1:2, there] = delta
            low = side_by_side(*lows, tok, True)
            ds_low = side_by_side(*ds_lows, tok, True)
            dq = dot(kt_scr[:, wide], ds_low)
            for half in range(2):
                dq_half = dq[:, half * tok : (half + 1) * tok]
                dq_out[p ^ (pair + half), :, head] = (dq_half.T * FACTOR).astype(BF16)
            own = slice((reach - pair) * tok, (reach + 2) * tok)
            dv = dot(low[own], grad)
            dk = dot(ds_low[own], query)
            done = pair * tok
            if pair:
                dv_out[0:done, head] += dv[:done]
                dk_out[0:done, head] += dk[:done]
            dv_out[done : done + 2 * tok, head] = dv[done:]
            dk_out[done : done + 2 * tok, head] = dk[done:]
        by_key = jnp.sum(acc_scr[...], axis=1, keepdims=True)
        row = jnp.sum(by_key * onehots[...].astype(F32), axis=0, keepdims=True)
        sums_out[...] += jnp.where(lax.broadcasted_iota(jnp.int32, (8, tok), 0) == at, row, 0.0)


def columns_kernel(reach, tok, chunk, lengths, qd, kvo, onehots, stats, bias_ref, dk_in, dv_in, *rest):
    k_scr, v_scr, dk_scr, dv_scr = rest[-4:]
    outs, extras = rest[-4 - reach : -4], rest[: -4 - reach]
    p, plane = place(reach)
    length = lengths[...]
    span = reach * tok
    k_scr[:, HEAD_DIM:] = onehots[span:]
    later, lane = masks(tok)

    @pl.loop(0, kvo.shape[2] // HEAD_DIM, unroll=True)
    def _(h):
        head = pl.ds(pl.multiple_of(h * HEAD_DIM, HEAD_DIM), HEAD_DIM)
        at = chunk * (kvo.shape[2] // HEAD_DIM) + h
        bias = bias_rows(bias_ref, p * (HEADS // reach) + at, tok)
        for blk in range(reach):
            rows = slice(blk * tok, (blk + 1) * tok)
            k_scr[rows, :HEAD_DIM] = kvo[p ^ blk, 0:tok, head]
            v_scr[rows] = kvo[p ^ blk, tok : 2 * tok, head]
        for pair in range(0, reach, 2):
            query, grad = query_pair(qd, p, pair, tok, head)
            wide = slice(pair * tok, span)
            logits = dot_nt(k_scr[wide], jnp.concatenate([query, bias], axis=1))
            probs_both = dot_nt(v_scr[wide], grad)
            lows, ds_lows = [], []
            for half in range(2):
                a = pair + half
                there = slice(a * tok, (a + 1) * tok)
                cols = slice(half * tok, (half + 1) * tok)
                live = (plane + 1) * span + a * tok + lane < length
                norm = jnp.where(live, stats[h, 0:1, there], -HIDDEN)
                delta = stats[h, 1:2, there]
                s = logits[half * tok :, cols] * (FACTOR * LOG2E)
                weight = jnp.exp2(s - norm)
                first = jnp.where(later, weight[:tok], 0.0)
                weight = jnp.concatenate([first, weight[tok:]], axis=0) if a < reach - 1 else first
                lows.append(weight.astype(BF16))
                ds_lows.append((weight * (probs_both[half * tok :, cols] - delta)).astype(BF16))
            dv = dot(side_by_side(*lows, tok, False), grad)
            dk = dot(side_by_side(*ds_lows, tok, False), query)
            if pair:
                dv_scr[wide] += dv
                dk_scr[wide] += dk
            else:
                dv_scr[...] = dv + dv_in[:, head]
                dk_scr[...] = dk + dk_in[:, head]
        for m in range(reach):
            mine = pl.ds(pl.multiple_of((p ^ m) * tok, tok), tok)
            outs[m][0:tok, head] = (dk_scr[mine] * FACTOR).astype(BF16)
            outs[m][tok : 2 * tok, head] = dv_scr[mine].astype(BF16)
            for at, dq in enumerate(extras):
                outs[m][(2 + at) * tok : (3 + at) * tok, head] = dq[m, :, head]


def attach_kernel(sums, *refs):
    messages, outs = refs[: len(refs) // 2], refs[len(refs) // 2 :]
    parts = [part.astype(F32) for part in three_parts(sums[...])]
    parts = [jnp.concatenate(parts[:2], axis=1), jnp.concatenate([parts[2], jnp.zeros_like(parts[2])], axis=1)]
    below = jnp.concatenate(parts, axis=0).astype(BF16)
    for message, out in zip(messages, outs):
        count = message.shape[0]
        out[:count] = message[...]
        out[count:] = below


def add_kernel(reach, tok, a, b, out):
    out[...] = a[...] + b[...]


def join(reach, tok, first, p, slots, out):
    heads = HEADS // reach
    found = []
    for slot in slots:
        rows = slot[first : first + PAD].astype(F32)
        found.append(rows[:8, :FIELDS] + rows[:8, tok : tok + FIELDS] + rows[8:, :FIELDS])
    for q in range(reach):
        part = found[0]
        for m in range(1, reach):
            part = jnp.where(p == q ^ m, found[m], part)
        out[q * heads : (q + 1) * heads] = part[:heads]


def params(mib, *semantics):
    return pltpu.CompilerParams(
        vmem_limit_bytes=mib * MIB, dimension_semantics=semantics if semantics else None
    )


def cost(flops, nbytes, trans=0):
    return pl.CostEstimate(flops=flops, bytes_accessed=nbytes, transcendentals=trans)


def in_hbm(*arrays):
    return [pltpu.with_memory_space_constraint(array, pltpu.HBM) for array in arrays]


def in_vmem(*arrays):
    return [pltpu.with_memory_space_constraint(array, pltpu.VMEM) for array in arrays]


def following(value, mark):
    return lax.optimization_barrier((value, mark))[0]


def swapped(value, axis, mask):
    count = lax.axis_size(axis)
    return lax.ppermute(value, axis, [(source, source ^ mask) for source in range(count)])


def passed_along(value, axis, steps):
    count = lax.axis_size(axis)
    first, last = max(0, -steps), min(count, count - steps)
    return lax.ppermute(value, axis, [(source, source + steps) for source in range(first, last)])


def shards(queries, keys, values, grad_out, lengths, fields, field_bias):
    tok = queries.shape[1]
    row_width = queries.shape[2]
    reach = WINDOW // tok
    group = HEADS // reach
    per = group // CHUNKS
    width = per * HEAD_DIM
    span = reach * tok
    length = jnp.broadcast_to(lengths[:, None], (1, tok))
    raw = in_hbm(queries, grad_out, keys, values)

    def vmem(shape, dtype=BF16):
        return pltpu.VMEM(shape, dtype)


    def pad(chunk):
        return 0 if chunk else PAD

    def pack(chunk):
        return pl.pallas_call(
            functools.partial(pack_kernel, reach, tok, width, chunk),
            in_specs=[ANY] * 5,
            out_specs=[VMEM] * reach,
            out_shape=[pltpu.VMEM((4 * tok + pad(chunk), width), BF16)] * reach,
            scratch_shapes=[
                pltpu.VMEM((1, tok), jnp.int32),
                pltpu.SemaphoreType.DMA((4 * reach + 1,)),
            ],
            compiler_params=params(2),
            cost_estimate=cost(0, 2 * MIB),
            name="pack",
        )(*raw, *in_hbm(fields))

    def local(kernel, name, flops, out_shape, *args, scratch=()):
        return pl.pallas_call(
            kernel,
            in_specs=[VMEM] * len(args),
            out_specs=[VMEM] * len(out_shape),
            out_shape=out_shape,
            scratch_shapes=scratch,
            compiler_params=params(12),
            cost_estimate=cost(flops, 2 * MIB),
            name=name,
        )(*in_vmem(*args))

    def gather(chunk, arrived):
        out = [vmem((reach, 2 * tok, width)), vmem((reach, 2 * tok + pad(chunk), width))]
        return local(functools.partial(gather_kernel, reach, tok), "gather", GATHER_FLOPS if chunk else 0, out, *arrived)

    def rows_of(chunk, qd, kvo, kvp, sums, *onehots):
        out = [
            vmem((reach, tok, width)),
            vmem((span, width), F32),
            vmem((span, width), F32),
            vmem((per, 2, span), F32),
            vmem((8, tok), F32),
        ]
        if chunk == 0:
            out = [vmem((2 * span, tok))] + out
        scratch = [
            pltpu.VMEM((2 * span, 2 * HEAD_DIM), BF16),
            pltpu.VMEM((2 * span, HEAD_DIM), BF16),
            pltpu.VMEM((HEAD_DIM, 2 * span), BF16),
            pltpu.VMEM((2 * span, tok), F32),
        ]
        kernel = functools.partial(rows_kernel, reach, tok, chunk)
        args = (length, qd, kvo, kvp, field_bias, sums, *onehots)
        return local(kernel, "rows", ROWS_FLOPS, out, *args, scratch=scratch)

    def columns_of(chunk, qd, kvo, onehots, stats, dk, dv, *extras):
        out = [vmem(((2 + len(extras)) * tok, width))] * reach
        scratch = [
            pltpu.VMEM((span, 2 * HEAD_DIM), BF16),
            pltpu.VMEM((span, HEAD_DIM), BF16),
            pltpu.VMEM((span, HEAD_DIM), F32),
            pltpu.VMEM((span, HEAD_DIM), F32),
        ]
        kernel = functools.partial(columns_kernel, reach, tok, chunk)
        args = (length, qd, kvo, onehots, stats, field_bias, dk, dv, *extras)
        return local(kernel, "columns", COLUMNS_FLOPS[chunk], out, *args, scratch=scratch)

    def add(a, b):
        return local(functools.partial(add_kernel, reach, tok), "add", 0, [vmem(a.shape, F32)], a, b)[0]

    packed = [list(pack(c)) for c in range(CHUNKS)]
    packed[0][0] = following(packed[0][0], packed[1][0])
    planes, before, after = [], [], []
    for c in range(CHUNKS):
        arrived = packed[c][:1] + [swapped(packed[c][m], "seq", m) for m in range(1, reach)]
        qd, kv = gather(c, arrived)
        planes.append((qd, kv))
        moved = passed_along(kv, "seq", reach), passed_along(qd, "seq", -reach)
        before.append(following(moved[0], moved[1]) if c == 0 else moved[0])
        after.append(moved[1])
    sums = jnp.zeros((8, tok), F32)
    pending, dqs, onehots = [], [], []
    for c in range(CHUNKS):
        *made, dq, dk, dv, stats, sums = rows_of(c, *planes[c], before[c], sums, *onehots)
        onehots = onehots or made
        dqs.append(dq)
        stats = passed_along(following(stats, after[c]), "seq", -reach)
        pending.append((after[c], planes[c][1], *onehots, stats, dk, dv))
    messages = [list(columns_of(0, *pending[0], *dqs))]
    messages.append(columns_of(1, *pending[1]))
    sums = following(sums, messages[0][0])
    mask = reach
    while mask < lax.axis_size("seq"):
        sums = add(sums, swapped(sums, "seq", mask))
        mask *= 2
    mask = 1
    while mask < lax.axis_size("dp"):
        sums = add(sums, swapped(sums, "dp", mask))
        mask *= 2
    out = [vmem((2 * tok + PAD, width))] * reach
    messages[1] = local(attach_kernel, "attach", 0, out, sums, *messages[1])
    parts = [[own[0]] + [swapped(own[m], "seq", m) for m in range(1, reach)] for own in messages]

    blocks = [((1, 0), (2, 0), (0, 0), (0, 1)), ((1, 1), (2, 1))]
    grads = []
    for c in range(CHUNKS):
        last = c == CHUNKS - 1
        kernel = finish_kernel if last else unpack_kernel
        out = [jax.ShapeDtypeStruct((1, tok, row_width), BF16)] * 3
        grads = pl.pallas_call(
            functools.partial(kernel, reach, tok, group * HEAD_DIM, blocks[c]),
            in_specs=[VMEM] * reach + [ANY] * len(grads),
            out_specs=[ANY] * 3 + [VMEM] * last,
            out_shape=out + [jax.ShapeDtypeStruct((HEADS, FIELDS), F32)] * last,
            scratch_shapes=[pltpu.SemaphoreType.DMA((len(blocks[c]) * reach,))],
            input_output_aliases={reach + at: at for at in range(len(grads))},
            compiler_params=params(2),
            cost_estimate=cost(0, 2 * MIB),
            name="unpack",
        )(*in_vmem(*parts[c]), *grads)
    return grads


def solution(mesh):
    return jax.shard_map(
        shards,
        mesh=mesh,
        in_specs=(
            P("dp", "seq", None),
            P("dp", "seq", None),
            P("dp", "seq", None),
            P("dp", "seq", None),
            P("dp"),
            P("dp", "seq"),
            P(),
        ),
        out_specs=(P("dp", "seq", None), P("dp", "seq", None), P("dp", "seq", None), P()),
        check_vma=False,
    )
```

```python
import functools

import jax
import jax.numpy as jnp
from jax import lax
from jax.experimental import pallas as pl
from jax.experimental.pallas import tpu as pltpu
from jax.sharding import PartitionSpec as P

HEADS = 16
HEAD_DIM = 128
WINDOW = 512
FIELDS = 64
FACTOR = HEAD_DIM ** (-0.5)
LOG2E = 1.4426950408889634
HIDDEN = -1e30
PAD = 16
CHUNKS = 2
MIB = 1 << 20
BF16, F32 = jnp.bfloat16, jnp.float32
ANY = pl.BlockSpec(memory_space=pl.ANY)
VMEM = pl.BlockSpec(memory_space=pltpu.VMEM)
GATHER_FLOPS, ROWS_FLOPS, COLUMNS_FLOPS = 2 * 10**9, 2 * 10**9, (4 * 10**9, 0)
NT = (((1,), (1,)), ((), ()))


def dot(a, b):
    return jnp.dot(a, b, preferred_element_type=F32)


def dot_nt(a, b):
    return lax.dot_general(a, b, NT, preferred_element_type=F32)


def place(reach):
    index = lax.axis_index("seq")
    return lax.rem(index, reach), lax.div(index, reach)


def pack_kernel(reach, tok, width, chunk, q, g, k, v, fields, *rest):
    outs, field_scr, sems = rest[:reach], rest[-2], rest[-1]
    p, _ = place(reach)
    field_copy = pltpu.make_async_copy(fields, field_scr, sems.at[4 * reach])
    field_copy.start()
    copies = []
    for m in list(range(1, reach)) + [0]:
        first = pl.multiple_of((p ^ m) * (HEADS // reach * HEAD_DIM) + chunk * width, 128)
        for at, src in enumerate((q, g, k, v)):
            dst = outs[m].at[pl.ds(at * tok, tok)]
            copies.append(pltpu.make_async_copy(src.at[0, :, pl.ds(first, width)], dst, sems.at[len(copies)]))
            copies[-1].start()
    field_copy.wait()
    row = jnp.concatenate([field_scr[...].astype(F32)] * (width // tok), axis=1)
    for out in outs:
        if out.shape[0] > 4 * tok:
            out[4 * tok :] = jnp.broadcast_to(row, (PAD, width)).astype(BF16)
    for copy in copies:
        copy.wait()


def gather_kernel(reach, tok, *refs):
    arrived, qd, kv = refs[:reach], *refs[reach:]
    for m in range(reach):
        qd[m] = arrived[m][: 2 * tok]
        kv[m] = arrived[m][2 * tok :]


def unpack_kernel(reach, tok, group_width, blocks, *rest):
    parts, outs, sems = rest[:reach], rest[-4:-1], rest[-1]
    p, _ = place(reach)
    width = parts[0].shape[1]
    copies = []
    for m in range(reach):
        for at, (which, chunk) in enumerate(blocks):
            first = pl.multiple_of((p ^ m) * group_width + chunk * width, 128)
            dst = outs[which].at[0, :, pl.ds(first, width)]
            copies.append(pltpu.make_async_copy(parts[m].at[pl.ds(at * tok, tok)], dst, sems.at[len(copies)]))
            copies[-1].start()
    for copy in copies:
        copy.wait()


def finish_kernel(reach, tok, group_width, blocks, *rest):
    total, sems, total_scr, total_sem = rest[-4:]
    join(reach, tok, len(blocks) * tok, place(reach)[0], rest[:reach], total_scr)
    copy = pltpu.make_async_copy(total_scr, total, total_sem)
    copy.start()
    unpack_kernel(reach, tok, group_width, blocks, *rest[:-4], sems)
    copy.wait()


def onehot_of(fields, slot, tok):
    row = fields[slot, 2 * tok : 2 * tok + PAD, 0:tok].astype(F32)[0:1]
    lane = lax.broadcasted_iota(jnp.int32, (tok, tok), 1)
    lane = jnp.where(lane < FIELDS, lane, lane - FIELDS).astype(F32)
    return jnp.where(jnp.broadcast_to(row, (tok, tok)).T == lane, 1.0, 0.0).astype(BF16)


def bias_rows(bias_ref, head, tok):
    table = bias_ref[...].astype(F32)
    at = lax.broadcasted_iota(jnp.int32, table.shape, 0)
    row = jnp.sum(jnp.where(at == head, table, 0.0), axis=0, keepdims=True) * (1.0 / FACTOR)
    high = row.astype(BF16).astype(F32)
    return jnp.broadcast_to(jnp.concatenate([high, row - high], axis=1), (2 * tok, tok)).astype(BF16)


def three_parts(x):
    high = x.astype(BF16)
    rest = x - high.astype(F32)
    mid = rest.astype(BF16)
    return high, mid, (rest - mid.astype(F32)).astype(BF16)


def masks(tok):
    key_at = lax.broadcasted_iota(jnp.int32, (tok, tok), 0)
    query_at = lax.broadcasted_iota(jnp.int32, (tok, tok), 1)
    return key_at > query_at, lax.broadcasted_iota(jnp.int32, (1, tok), 1)


def query_pair(qd, p, a, tok, head):
    slots = (p ^ a, p ^ (a + 1))
    query = jnp.concatenate([qd[slot, 0:tok, head] for slot in slots], axis=0)
    grad = jnp.concatenate([qd[slot, tok : 2 * tok, head] for slot in slots], axis=0)
    return query, grad


def side_by_side(first, second, tok, ends):
    gap = jnp.zeros((tok, tok), first.dtype)
    first = jnp.concatenate([first, gap], axis=0) if ends else first
    return jnp.concatenate([first, jnp.concatenate([gap, second], axis=0)], axis=1)


def rows_kernel(reach, tok, chunk, lengths, qd, kvo, kvp, bias_ref, sums_in, *rest):
    *onehots, dq_out, dk_out, dv_out, stats_out, sums_out, k_scr, v_scr, kt_scr, acc_scr = rest
    onehots = onehots[0]
    p, plane = place(reach)
    length = lengths[...]
    span = reach * tok

    for blk in range(2 * reach):
        rows = slice(blk * tok, (blk + 1) * tok)
        if chunk == 0:
            onehots[rows] = onehot_of(kvp if blk < reach else kvo, p ^ (blk % reach), tok)
        k_scr[rows, HEAD_DIM:] = onehots[rows]
    per = kvo.shape[2] // HEAD_DIM
    sums_out[...] = sums_in[...]
    shut = jnp.where(plane == 0, HIDDEN, 0.0).astype(F32)
    later, lane = masks(tok)

    @pl.loop(0, kvo.shape[2] // HEAD_DIM, unroll=True)
    def _(h):
        head = pl.ds(pl.multiple_of(h * HEAD_DIM, HEAD_DIM), HEAD_DIM)
        at = chunk * per + h
        bias = bias_rows(bias_ref, p * (HEADS // reach) + at, tok)
        for blk in range(2 * reach):
            rows = slice(blk * tok, (blk + 1) * tok)
            src, slot = (kvp if blk < reach else kvo), p ^ (blk % reach)
            key = src[slot, 0:tok, head]
            k_scr[rows, :HEAD_DIM] = key
            kt_scr[:, rows] = key.T
            v_scr[rows] = src[slot, tok : 2 * tok, head]
        acc_scr[...] = jnp.zeros_like(acc_scr)
        for pair in range(0, reach, 2):
            query, grad = query_pair(qd, p, pair, tok, head)
            wide = slice(pair * tok, (pair + reach + 2) * tok)
            logits = dot_nt(k_scr[wide], jnp.concatenate([query, bias], axis=1))
            probs_both = dot_nt(v_scr[wide], grad)
            lows, ds_lows = [], []
            for half in range(2):
                a = pair + half
                rows = slice(a * tok, (a + reach + 1) * tok)
                mine = slice(half * tok, (half + reach + 1) * tok)
                there = slice(a * tok, (a + 1) * tok)
                cols = slice(half * tok, (half + 1) * tok)
                s = logits[mine, cols] * (FACTOR * LOG2E)
                seen = [jnp.where(later, s[:tok], HIDDEN) + shut, s[tok : (reach - a) * tok] + shut]
                seen += [s[(reach - a) * tok : -tok], jnp.where(later, HIDDEN, s[-tok:])]
                s = jnp.concatenate([part for part in seen if part.shape[0]], axis=0)
                peak = jnp.max(s, axis=0, keepdims=True)
                power = jnp.exp2(s - peak)
                total = jnp.sum(power, axis=0, keepdims=True)
                live = plane * span + a * tok + lane < length
                weight = power * jnp.where(live, 1.0 / total, 0.0)
                low = weight.astype(BF16)
                probs = probs_both[mine, cols]
                delta = jnp.sum(low.astype(F32) * probs, axis=0, keepdims=True)
                ds = weight * (probs - delta)
                acc_scr[rows] += ds
                lows.append(low)
                ds_lows.append(ds.astype(BF16))
                stats_out[h, 0:1, there] = peak + jnp.log2(total)
                stats_out[h, 1:2, there] = delta
            low = side_by_side(*lows, tok, True)
            ds_low = side_by_side(*ds_lows, tok, True)
            dq = dot(kt_scr[:, wide], ds_low)
            for half in range(2):
                dq_half = dq[:, half * tok : (half + 1) * tok]
                dq_out[p ^ (pair + half), :, head] = (dq_half.T * FACTOR).astype(BF16)
            own = slice((reach - pair) * tok, (reach + 2) * tok)
            dv = dot(low[own], grad)
            dk = dot(ds_low[own], query)
            done = pair * tok
            if pair:
                dv_out[0:done, head] += dv[:done]
                dk_out[0:done, head] += dk[:done]
            dv_out[done : done + 2 * tok, head] = dv[done:]
            dk_out[done : done + 2 * tok, head] = dk[done:]
        by_key = jnp.sum(acc_scr[...], axis=1, keepdims=True)
        row = jnp.sum(by_key * onehots[...].astype(F32), axis=0, keepdims=True)
        sums_out[...] += jnp.where(lax.broadcasted_iota(jnp.int32, (8, tok), 0) == at, row, 0.0)


def columns_kernel(reach, tok, chunk, lengths, qd, kvo, onehots, stats, bias_ref, dk_in, dv_in, *rest):
    k_scr, v_scr, dk_scr, dv_scr = rest[-4:]
    outs, extras = rest[-4 - reach : -4], rest[: -4 - reach]
    p, plane = place(reach)
    length = lengths[...]
    span = reach * tok
    k_scr[:, HEAD_DIM:] = onehots[span:]
    later, lane = masks(tok)

    @pl.loop(0, kvo.shape[2] // HEAD_DIM, unroll=True)
    def _(h):
        head = pl.ds(pl.multiple_of(h * HEAD_DIM, HEAD_DIM), HEAD_DIM)
        at = chunk * (kvo.shape[2] // HEAD_DIM) + h
        bias = bias_rows(bias_ref, p * (HEADS // reach) + at, tok)
        for blk in range(reach):
            rows = slice(blk * tok, (blk + 1) * tok)
            k_scr[rows, :HEAD_DIM] = kvo[p ^ blk, 0:tok, head]
            v_scr[rows] = kvo[p ^ blk, tok : 2 * tok, head]
        for pair in range(0, reach, 2):
            query, grad = query_pair(qd, p, pair, tok, head)
            wide = slice(pair * tok, span)
            logits = dot_nt(k_scr[wide], jnp.concatenate([query, bias], axis=1))
            probs_both = dot_nt(v_scr[wide], grad)
            lows, ds_lows = [], []
            for half in range(2):
                a = pair + half
                there = slice(a * tok, (a + 1) * tok)
                cols = slice(half * tok, (half + 1) * tok)
                live = (plane + 1) * span + a * tok + lane < length
                norm = jnp.where(live, stats[h, 0:1, there], -HIDDEN)
                delta = stats[h, 1:2, there]
                s = logits[half * tok :, cols] * (FACTOR * LOG2E)
                weight = jnp.exp2(s - norm)
                first = jnp.where(later, weight[:tok], 0.0)
                weight = jnp.concatenate([first, weight[tok:]], axis=0) if a < reach - 1 else first
                lows.append(weight.astype(BF16))
                ds_lows.append((weight * (probs_both[half * tok :, cols] - delta)).astype(BF16))
            dv = dot(side_by_side(*lows, tok, False), grad)
            dk = dot(side_by_side(*ds_lows, tok, False), query)
            if pair:
                dv_scr[wide] += dv
                dk_scr[wide] += dk
            else:
                dv_scr[...] = dv + dv_in[:, head]
                dk_scr[...] = dk + dk_in[:, head]
        for m in range(reach):
            mine = pl.ds(pl.multiple_of((p ^ m) * tok, tok), tok)
            outs[m][0:tok, head] = (dk_scr[mine] * FACTOR).astype(BF16)
            outs[m][tok : 2 * tok, head] = dv_scr[mine].astype(BF16)
            for at, dq in enumerate(extras):
                outs[m][(2 + at) * tok : (3 + at) * tok, head] = dq[m, :, head]


def attach_kernel(sums, *refs):
    messages, outs = refs[: len(refs) // 2], refs[len(refs) // 2 :]
    parts = [part.astype(F32) for part in three_parts(sums[...])]
    parts = [jnp.concatenate(parts[:2], axis=1), jnp.concatenate([parts[2], jnp.zeros_like(parts[2])], axis=1)]
    below = jnp.concatenate(parts, axis=0).astype(BF16)
    for message, out in zip(messages, outs):
        count = message.shape[0]
        out[:count] = message[...]
        out[count:] = below


def add_kernel(reach, tok, a, b, out):
    out[...] = a[...] + b[...]


def join(reach, tok, first, p, slots, out):
    heads = HEADS // reach
    found = []
    for slot in slots:
        rows = slot[first : first + PAD].astype(F32)
        found.append(rows[:8, :FIELDS] + rows[:8, tok : tok + FIELDS] + rows[8:, :FIELDS])
    for q in range(reach):
        part = found[0]
        for m in range(1, reach):
            part = jnp.where(p == q ^ m, found[m], part)
        out[q * heads : (q + 1) * heads] = part[:heads]


def params(mib, *semantics):
    return pltpu.CompilerParams(
        vmem_limit_bytes=mib * MIB, dimension_semantics=semantics if semantics else None
    )


def cost(flops, nbytes, trans=0):
    return pl.CostEstimate(flops=flops, bytes_accessed=nbytes, transcendentals=trans)


def in_hbm(*arrays):
    return [pltpu.with_memory_space_constraint(array, pltpu.HBM) for array in arrays]


def in_vmem(*arrays):
    return [pltpu.with_memory_space_constraint(array, pltpu.VMEM) for array in arrays]


def following(value, mark):
    return lax.optimization_barrier((value, mark))[0]


def swapped(value, axis, mask):
    count = lax.axis_size(axis)
    return lax.ppermute(value, axis, [(source, source ^ mask) for source in range(count)])


def passed_along(value, axis, steps):
    count = lax.axis_size(axis)
    first, last = max(0, -steps), min(count, count - steps)
    return lax.ppermute(value, axis, [(source, source + steps) for source in range(first, last)])


def shards(queries, keys, values, grad_out, lengths, fields, field_bias):
    tok = queries.shape[1]
    row_width = queries.shape[2]
    reach = WINDOW // tok
    group = HEADS // reach
    per = group // CHUNKS
    width = per * HEAD_DIM
    span = reach * tok
    length = jnp.broadcast_to(lengths[:, None], (1, tok))
    raw = in_hbm(queries, grad_out, keys, values)

    def vmem(shape, dtype=BF16):
        return pltpu.VMEM(shape, dtype)


    def pad(chunk):
        return 0 if chunk else PAD

    def pack(chunk):
        return pl.pallas_call(
            functools.partial(pack_kernel, reach, tok, width, chunk),
            in_specs=[ANY] * 5,
            out_specs=[VMEM] * reach,
            out_shape=[pltpu.VMEM((4 * tok + pad(chunk), width), BF16)] * reach,
            scratch_shapes=[
                pltpu.VMEM((1, tok), jnp.int32),
                pltpu.SemaphoreType.DMA((4 * reach + 1,)),
            ],
            compiler_params=params(2),
            cost_estimate=cost(0, 2 * MIB),
            name="pack",
        )(*raw, *in_hbm(fields))

    def local(kernel, name, flops, out_shape, *args, scratch=()):
        return pl.pallas_call(
            kernel,
            in_specs=[VMEM] * len(args),
            out_specs=[VMEM] * len(out_shape),
            out_shape=out_shape,
            scratch_shapes=scratch,
            compiler_params=params(12),
            cost_estimate=cost(flops, 2 * MIB),
            name=name,
        )(*in_vmem(*args))

    def gather(chunk, arrived):
        out = [vmem((reach, 2 * tok, width)), vmem((reach, 2 * tok + pad(chunk), width))]
        return local(functools.partial(gather_kernel, reach, tok), "gather", GATHER_FLOPS if chunk else 0, out, *arrived)

    def rows_of(chunk, qd, kvo, kvp, sums, *onehots):
        out = [
            vmem((reach, tok, width)),
            vmem((span, width), F32),
            vmem((span, width), F32),
            vmem((per, 2, span), F32),
            vmem((8, tok), F32),
        ]
        if chunk == 0:
            out = [vmem((2 * span, tok))] + out
        scratch = [
            pltpu.VMEM((2 * span, 2 * HEAD_DIM), BF16),
            pltpu.VMEM((2 * span, HEAD_DIM), BF16),
            pltpu.VMEM((HEAD_DIM, 2 * span), BF16),
            pltpu.VMEM((2 * span, tok), F32),
        ]
        kernel = functools.partial(rows_kernel, reach, tok, chunk)
        args = (length, qd, kvo, kvp, field_bias, sums, *onehots)
        return local(kernel, "rows", ROWS_FLOPS, out, *args, scratch=scratch)

    def columns_of(chunk, qd, kvo, onehots, stats, dk, dv, *extras):
        out = [vmem(((2 + len(extras)) * tok, width))] * reach
        scratch = [
            pltpu.VMEM((span, 2 * HEAD_DIM), BF16),
            pltpu.VMEM((span, HEAD_DIM), BF16),
            pltpu.VMEM((span, HEAD_DIM), F32),
            pltpu.VMEM((span, HEAD_DIM), F32),
        ]
        kernel = functools.partial(columns_kernel, reach, tok, chunk)
        args = (length, qd, kvo, onehots, stats, field_bias, dk, dv, *extras)
        return local(kernel, "columns", COLUMNS_FLOPS[chunk], out, *args, scratch=scratch)

    def add(a, b):
        return local(functools.partial(add_kernel, reach, tok), "add", 0, [vmem(a.shape, F32)], a, b)[0]

    packed = [list(pack(c)) for c in range(CHUNKS)]
    packed[0][0] = following(packed[0][0], packed[1][0])
    planes, before, after = [], [], []
    for c in range(CHUNKS):
        arrived = packed[c][:1] + [swapped(packed[c][m], "seq", m) for m in range(1, reach)]
        qd, kv = gather(c, arrived)
        planes.append((qd, kv))
        moved = passed_along(kv, "seq", reach), passed_along(qd, "seq", -reach)
        before.append(following(moved[0], moved[1]) if c == 0 else moved[0])
        after.append(moved[1])
    sums = jnp.zeros((8, tok), F32)
    pending, dqs, onehots = [], [], []
    for c in range(CHUNKS):
        *made, dq, dk, dv, stats, sums = rows_of(c, *planes[c], before[c], sums, *onehots)
        onehots = onehots or made
        dqs.append(dq)
        stats = passed_along(following(stats, after[c]), "seq", -reach)
        pending.append((after[c], planes[c][1], *onehots, stats, dk, dv))
    messages = [list(columns_of(0, *pending[0], *dqs))]
    messages.append(columns_of(1, *pending[1]))
    sums = following(sums, messages[0][0])
    mask = reach
    while mask < lax.axis_size("seq"):
        sums = add(sums, swapped(sums, "seq", mask))
        mask *= 2
    mask = 1
    while mask < lax.axis_size("dp"):
        sums = add(sums, swapped(sums, "dp", mask))
        mask *= 2
    out = [vmem((2 * tok + PAD, width))] * reach
    messages[1] = local(attach_kernel, "attach", 0, out, sums, *messages[1])
    parts = [[own[0]] + [swapped(own[m], "seq", m) for m in range(1, reach)] for own in messages]

    blocks = [((1, 0), (2, 0), (0, 0), (0, 1)), ((1, 1), (2, 1))]
    grads = []
    for c in range(CHUNKS):
        last = c == CHUNKS - 1
        kernel = finish_kernel if last else unpack_kernel
        out = [jax.ShapeDtypeStruct((1, tok, row_width), BF16)] * 3
        grads = pl.pallas_call(
            functools.partial(kernel, reach, tok, group * HEAD_DIM, blocks[c]),
            in_specs=[VMEM] * reach + [ANY] * len(grads),
            out_specs=[ANY] * (3 + last),
            out_shape=out + [jax.ShapeDtypeStruct((HEADS, FIELDS), F32)] * last,
            scratch_shapes=[pltpu.SemaphoreType.DMA((len(blocks[c]) * reach,))]
            + [pltpu.VMEM((HEADS, FIELDS), F32), pltpu.SemaphoreType.DMA] * last,
            input_output_aliases={reach + at: at for at in range(len(grads))},
            compiler_params=params(2),
            cost_estimate=cost(0, 2 * MIB),
            name="unpack",
        )(*in_vmem(*parts[c]), *grads)
    return grads


def solution(mesh):
    return jax.shard_map(
        shards,
        mesh=mesh,
        in_specs=(
            P("dp", "seq", None),
            P("dp", "seq", None),
            P("dp", "seq", None),
            P("dp", "seq", None),
            P("dp"),
            P("dp", "seq"),
            P(),
        ),
        out_specs=(P("dp", "seq", None), P("dp", "seq", None), P("dp", "seq", None), P()),
        check_vma=False,
    )
```

```python
import functools

import jax
import jax.numpy as jnp
from jax import lax
from jax.experimental import pallas as pl
from jax.experimental.pallas import tpu as pltpu
from jax.sharding import PartitionSpec as P

HEADS = 16
HEAD_DIM = 128
WINDOW = 512
FIELDS = 64
FACTOR = HEAD_DIM ** (-0.5)
LOG2E = 1.4426950408889634
HIDDEN = -1e30
PAD = 16
CHUNKS = 2
MIB = 1 << 20
BF16, F32 = jnp.bfloat16, jnp.float32
ANY = pl.BlockSpec(memory_space=pl.ANY)
VMEM = pl.BlockSpec(memory_space=pltpu.VMEM)
GATHER_FLOPS, ROWS_FLOPS, COLUMNS_FLOPS = 2 * 10**9, 2 * 10**9, (4 * 10**9, 0)
NT = (((1,), (1,)), ((), ()))


def dot(a, b):
    return jnp.dot(a, b, preferred_element_type=F32)


def dot_nt(a, b):
    return lax.dot_general(a, b, NT, preferred_element_type=F32)


def place(reach):
    index = lax.axis_index("seq")
    return lax.rem(index, reach), lax.div(index, reach)


def pack_kernel(reach, tok, width, wanted, q, g, k, v, fields, *rest):
    outs, field_scr, sems = rest[: len(wanted)], rest[-2], rest[-1]
    p, _ = place(reach)
    field_copy = pltpu.make_async_copy(fields, field_scr, sems.at[4 * len(wanted)])
    field_copy.start()
    copies = []
    for out, (m, chunk) in zip(outs, wanted):
        first = pl.multiple_of((p ^ m) * (HEADS // reach * HEAD_DIM) + chunk * width, 128)
        for at, src in enumerate((q, g, k, v)):
            dst = out.at[pl.ds(at * tok, tok)]
            copies.append(pltpu.make_async_copy(src.at[0, :, pl.ds(first, width)], dst, sems.at[len(copies)]))
            copies[-1].start()
    field_copy.wait()
    row = jnp.concatenate([field_scr[...].astype(F32)] * (width // tok), axis=1)
    for out in outs:
        if out.shape[0] > 4 * tok:
            out[4 * tok :] = jnp.broadcast_to(row, (PAD, width)).astype(BF16)
    for copy in copies:
        copy.wait()


def gather_kernel(reach, tok, *refs):
    arrived, qd, kv = refs[:reach], *refs[reach:]
    for m in range(reach):
        qd[m] = arrived[m][: 2 * tok]
        kv[m] = arrived[m][2 * tok :]


def unpack_kernel(reach, tok, group_width, moves, *rest):
    outs, sems = rest[-4:-1], rest[-1]
    p, _ = place(reach)
    width = rest[0].shape[1]
    copies = []
    for i, m, at, which, chunk in moves:
        first = pl.multiple_of((p ^ m) * group_width + chunk * width, 128)
        dst = outs[which].at[0, :, pl.ds(first, width)]
        copies.append(pltpu.make_async_copy(rest[i].at[pl.ds(at * tok, tok)], dst, sems.at[len(copies)]))
        copies[-1].start()
    for copy in copies:
        copy.wait()


def finish_kernel(reach, tok, group_width, moves, *rest):
    total, sems, total_scr, total_sem = rest[-4:]
    join(reach, tok, 2 * tok, place(reach)[0], rest[:reach], total_scr)
    copy = pltpu.make_async_copy(total_scr, total, total_sem)
    copy.start()
    unpack_kernel(reach, tok, group_width, moves, *rest[:-4], sems)
    copy.wait()


def onehot_of(fields, slot, tok):
    row = fields[slot, 2 * tok : 2 * tok + PAD, 0:tok].astype(F32)[0:1]
    lane = lax.broadcasted_iota(jnp.int32, (tok, tok), 1)
    lane = jnp.where(lane < FIELDS, lane, lane - FIELDS).astype(F32)
    return jnp.where(jnp.broadcast_to(row, (tok, tok)).T == lane, 1.0, 0.0).astype(BF16)


def bias_rows(bias_ref, head, tok):
    table = bias_ref[...].astype(F32)
    at = lax.broadcasted_iota(jnp.int32, table.shape, 0)
    row = jnp.sum(jnp.where(at == head, table, 0.0), axis=0, keepdims=True) * (1.0 / FACTOR)
    high = row.astype(BF16).astype(F32)
    return jnp.broadcast_to(jnp.concatenate([high, row - high], axis=1), (2 * tok, tok)).astype(BF16)


def three_parts(x):
    high = x.astype(BF16)
    rest = x - high.astype(F32)
    mid = rest.astype(BF16)
    return high, mid, (rest - mid.astype(F32)).astype(BF16)


def masks(tok):
    key_at = lax.broadcasted_iota(jnp.int32, (tok, tok), 0)
    query_at = lax.broadcasted_iota(jnp.int32, (tok, tok), 1)
    return key_at > query_at, lax.broadcasted_iota(jnp.int32, (1, tok), 1)


def query_pair(qd, p, a, tok, head):
    slots = (p ^ a, p ^ (a + 1))
    query = jnp.concatenate([qd[slot, 0:tok, head] for slot in slots], axis=0)
    grad = jnp.concatenate([qd[slot, tok : 2 * tok, head] for slot in slots], axis=0)
    return query, grad


def side_by_side(first, second, tok, ends):
    gap = jnp.zeros((tok, tok), first.dtype)
    first = jnp.concatenate([first, gap], axis=0) if ends else first
    return jnp.concatenate([first, jnp.concatenate([gap, second], axis=0)], axis=1)


def rows_kernel(reach, tok, chunk, lengths, qd, kvo, kvp, bias_ref, sums_in, *rest):
    *onehots, dq_out, dk_out, dv_out, stats_out, sums_out, k_scr, v_scr, kt_scr, acc_scr = rest
    onehots = onehots[0]
    p, plane = place(reach)
    length = lengths[...]
    span = reach * tok

    for blk in range(2 * reach):
        rows = slice(blk * tok, (blk + 1) * tok)
        if chunk == 0:
            onehots[rows] = onehot_of(kvp if blk < reach else kvo, p ^ (blk % reach), tok)
        k_scr[rows, HEAD_DIM:] = onehots[rows]
    per = kvo.shape[2] // HEAD_DIM
    sums_out[...] = sums_in[...]
    shut = jnp.where(plane == 0, HIDDEN, 0.0).astype(F32)
    later, lane = masks(tok)

    @pl.loop(0, kvo.shape[2] // HEAD_DIM, unroll=True)
    def _(h):
        head = pl.ds(pl.multiple_of(h * HEAD_DIM, HEAD_DIM), HEAD_DIM)
        at = chunk * per + h
        bias = bias_rows(bias_ref, p * (HEADS // reach) + at, tok)
        for blk in range(2 * reach):
            rows = slice(blk * tok, (blk + 1) * tok)
            src, slot = (kvp if blk < reach else kvo), p ^ (blk % reach)
            key = src[slot, 0:tok, head]
            k_scr[rows, :HEAD_DIM] = key
            kt_scr[:, rows] = key.T
            v_scr[rows] = src[slot, tok : 2 * tok, head]
        acc_scr[...] = jnp.zeros_like(acc_scr)
        for pair in range(0, reach, 2):
            query, grad = query_pair(qd, p, pair, tok, head)
            wide = slice(pair * tok, (pair + reach + 2) * tok)
            logits = dot_nt(k_scr[wide], jnp.concatenate([query, bias], axis=1))
            probs_both = dot_nt(v_scr[wide], grad)
            lows, ds_lows = [], []
            for half in range(2):
                a = pair + half
                rows = slice(a * tok, (a + reach + 1) * tok)
                mine = slice(half * tok, (half + reach + 1) * tok)
                there = slice(a * tok, (a + 1) * tok)
                cols = slice(half * tok, (half + 1) * tok)
                s = logits[mine, cols] * (FACTOR * LOG2E)
                seen = [jnp.where(later, s[:tok], HIDDEN) + shut, s[tok : (reach - a) * tok] + shut]
                seen += [s[(reach - a) * tok : -tok], jnp.where(later, HIDDEN, s[-tok:])]
                s = jnp.concatenate([part for part in seen if part.shape[0]], axis=0)
                peak = jnp.max(s, axis=0, keepdims=True)
                power = jnp.exp2(s - peak)
                total = jnp.sum(power, axis=0, keepdims=True)
                live = plane * span + a * tok + lane < length
                weight = power * jnp.where(live, 1.0 / total, 0.0)
                low = weight.astype(BF16)
                probs = probs_both[mine, cols]
                delta = jnp.sum(low.astype(F32) * probs, axis=0, keepdims=True)
                ds = weight * (probs - delta)
                acc_scr[rows] += ds
                lows.append(low)
                ds_lows.append(ds.astype(BF16))
                stats_out[h, 0:1, there] = peak + jnp.log2(total)
                stats_out[h, 1:2, there] = delta
            low = side_by_side(*lows, tok, True)
            ds_low = side_by_side(*ds_lows, tok, True)
            dq = dot(kt_scr[:, wide], ds_low)
            for half in range(2):
                dq_half = dq[:, half * tok : (half + 1) * tok]
                dq_out[p ^ (pair + half), :, head] = (dq_half.T * FACTOR).astype(BF16)
            own = slice((reach - pair) * tok, (reach + 2) * tok)
            dv = dot(low[own], grad)
            dk = dot(ds_low[own], query)
            done = pair * tok
            if pair:
                dv_out[0:done, head] += dv[:done]
                dk_out[0:done, head] += dk[:done]
            dv_out[done : done + 2 * tok, head] = dv[done:]
            dk_out[done : done + 2 * tok, head] = dk[done:]
        by_key = jnp.sum(acc_scr[...], axis=1, keepdims=True)
        row = jnp.sum(by_key * onehots[...].astype(F32), axis=0, keepdims=True)
        sums_out[...] += jnp.where(lax.broadcasted_iota(jnp.int32, (8, tok), 0) == at, row, 0.0)


def columns_kernel(reach, tok, chunk, lengths, qd, kvo, onehots, stats, bias_ref, dk_in, dv_in, *rest):
    k_scr, v_scr, dk_scr, dv_scr = rest[-4:]
    outs, extras = rest[-4 - reach : -4], rest[: -4 - reach]
    p, plane = place(reach)
    length = lengths[...]
    span = reach * tok
    k_scr[:, HEAD_DIM:] = onehots[span:]
    later, lane = masks(tok)

    @pl.loop(0, kvo.shape[2] // HEAD_DIM, unroll=True)
    def _(h):
        head = pl.ds(pl.multiple_of(h * HEAD_DIM, HEAD_DIM), HEAD_DIM)
        at = chunk * (kvo.shape[2] // HEAD_DIM) + h
        bias = bias_rows(bias_ref, p * (HEADS // reach) + at, tok)
        for blk in range(reach):
            rows = slice(blk * tok, (blk + 1) * tok)
            k_scr[rows, :HEAD_DIM] = kvo[p ^ blk, 0:tok, head]
            v_scr[rows] = kvo[p ^ blk, tok : 2 * tok, head]
        for pair in range(0, reach, 2):
            query, grad = query_pair(qd, p, pair, tok, head)
            wide = slice(pair * tok, span)
            logits = dot_nt(k_scr[wide], jnp.concatenate([query, bias], axis=1))
            probs_both = dot_nt(v_scr[wide], grad)
            lows, ds_lows = [], []
            for half in range(2):
                a = pair + half
                there = slice(a * tok, (a + 1) * tok)
                cols = slice(half * tok, (half + 1) * tok)
                live = (plane + 1) * span + a * tok + lane < length
                norm = jnp.where(live, stats[h, 0:1, there], -HIDDEN)
                delta = stats[h, 1:2, there]
                s = logits[half * tok :, cols] * (FACTOR * LOG2E)
                weight = jnp.exp2(s - norm)
                first = jnp.where(later, weight[:tok], 0.0)
                weight = jnp.concatenate([first, weight[tok:]], axis=0) if a < reach - 1 else first
                lows.append(weight.astype(BF16))
                ds_lows.append((weight * (probs_both[half * tok :, cols] - delta)).astype(BF16))
            dv = dot(side_by_side(*lows, tok, False), grad)
            dk = dot(side_by_side(*ds_lows, tok, False), query)
            if pair:
                dv_scr[wide] += dv
                dk_scr[wide] += dk
            else:
                dv_scr[...] = dv + dv_in[:, head]
                dk_scr[...] = dk + dk_in[:, head]
        for m in range(reach):
            mine = pl.ds(pl.multiple_of((p ^ m) * tok, tok), tok)
            outs[m][0:tok, head] = (dk_scr[mine] * FACTOR).astype(BF16)
            outs[m][tok : 2 * tok, head] = dv_scr[mine].astype(BF16)
            for at, dq in enumerate(extras):
                outs[m][(2 + at) * tok : (3 + at) * tok, head] = dq[m, :, head]


def attach_kernel(sums, *refs):
    messages, outs = refs[: len(refs) // 2], refs[len(refs) // 2 :]
    parts = [part.astype(F32) for part in three_parts(sums[...])]
    parts = [jnp.concatenate(parts[:2], axis=1), jnp.concatenate([parts[2], jnp.zeros_like(parts[2])], axis=1)]
    below = jnp.concatenate(parts, axis=0).astype(BF16)
    for message, out in zip(messages, outs):
        count = message.shape[0]
        out[:count] = message[...]
        out[count:] = below


def add_kernel(reach, tok, a, b, out):
    out[...] = a[...] + b[...]


def join(reach, tok, first, p, slots, out):
    heads = HEADS // reach
    found = []
    for slot in slots:
        rows = slot[first : first + PAD].astype(F32)
        found.append(rows[:8, :FIELDS] + rows[:8, tok : tok + FIELDS] + rows[8:, :FIELDS])
    for q in range(reach):
        part = found[0]
        for m in range(1, reach):
            part = jnp.where(p == q ^ m, found[m], part)
        out[q * heads : (q + 1) * heads] = part[:heads]


def params(mib, *semantics):
    return pltpu.CompilerParams(
        vmem_limit_bytes=mib * MIB, dimension_semantics=semantics if semantics else None
    )


def cost(flops, nbytes, trans=0):
    return pl.CostEstimate(flops=flops, bytes_accessed=nbytes, transcendentals=trans)


def in_hbm(*arrays):
    return [pltpu.with_memory_space_constraint(array, pltpu.HBM) for array in arrays]


def in_vmem(*arrays):
    return [pltpu.with_memory_space_constraint(array, pltpu.VMEM) for array in arrays]


def following(value, mark):
    return lax.optimization_barrier((value, mark))[0]


def swapped(value, axis, mask):
    count = lax.axis_size(axis)
    return lax.ppermute(value, axis, [(source, source ^ mask) for source in range(count)])


def passed_along(value, axis, steps):
    count = lax.axis_size(axis)
    first, last = max(0, -steps), min(count, count - steps)
    return lax.ppermute(value, axis, [(source, source + steps) for source in range(first, last)])


def shards(queries, keys, values, grad_out, lengths, fields, field_bias):
    tok = queries.shape[1]
    row_width = queries.shape[2]
    reach = WINDOW // tok
    group = HEADS // reach
    per = group // CHUNKS
    width = per * HEAD_DIM
    span = reach * tok
    length = jnp.broadcast_to(lengths[:, None], (1, tok))
    raw = in_hbm(queries, grad_out, keys, values)

    def vmem(shape, dtype=BF16):
        return pltpu.VMEM(shape, dtype)


    def pad(chunk):
        return 0 if chunk else PAD

    def pack(wanted):
        return pl.pallas_call(
            functools.partial(pack_kernel, reach, tok, width, wanted),
            in_specs=[ANY] * 5,
            out_specs=[VMEM] * len(wanted),
            out_shape=[vmem((4 * tok + pad(chunk), width)) for _, chunk in wanted],
            scratch_shapes=[
                pltpu.VMEM((1, tok), jnp.int32),
                pltpu.SemaphoreType.DMA((4 * len(wanted) + 1,)),
            ],
            compiler_params=params(2),
            cost_estimate=cost(0, 2 * MIB),
            name="pack",
        )(*raw, *in_hbm(fields))

    def local(kernel, name, flops, out_shape, *args, scratch=()):
        return pl.pallas_call(
            kernel,
            in_specs=[VMEM] * len(args),
            out_specs=[VMEM] * len(out_shape),
            out_shape=out_shape,
            scratch_shapes=scratch,
            compiler_params=params(12),
            cost_estimate=cost(flops, 2 * MIB),
            name=name,
        )(*in_vmem(*args))

    def gather(chunk, arrived):
        out = [vmem((reach, 2 * tok, width)), vmem((reach, 2 * tok + pad(chunk), width))]
        return local(functools.partial(gather_kernel, reach, tok), "gather", GATHER_FLOPS if chunk else 0, out, *arrived)

    def rows_of(chunk, qd, kvo, kvp, sums, *onehots):
        out = [
            vmem((reach, tok, width)),
            vmem((span, width), F32),
            vmem((span, width), F32),
            vmem((per, 2, span), F32),
            vmem((8, tok), F32),
        ]
        if chunk == 0:
            out = [vmem((2 * span, tok))] + out
        scratch = [
            pltpu.VMEM((2 * span, 2 * HEAD_DIM), BF16),
            pltpu.VMEM((2 * span, HEAD_DIM), BF16),
            pltpu.VMEM((HEAD_DIM, 2 * span), BF16),
            pltpu.VMEM((2 * span, tok), F32),
        ]
        kernel = functools.partial(rows_kernel, reach, tok, chunk)
        args = (length, qd, kvo, kvp, field_bias, sums, *onehots)
        return local(kernel, "rows", ROWS_FLOPS, out, *args, scratch=scratch)

    def columns_of(chunk, qd, kvo, onehots, stats, dk, dv, *extras):
        out = [vmem(((2 + len(extras)) * tok, width))] * reach
        scratch = [
            pltpu.VMEM((span, 2 * HEAD_DIM), BF16),
            pltpu.VMEM((span, HEAD_DIM), BF16),
            pltpu.VMEM((span, HEAD_DIM), F32),
            pltpu.VMEM((span, HEAD_DIM), F32),
        ]
        kernel = functools.partial(columns_kernel, reach, tok, chunk)
        args = (length, qd, kvo, onehots, stats, field_bias, dk, dv, *extras)
        return local(kernel, "columns", COLUMNS_FLOPS[chunk], out, *args, scratch=scratch)

    def add(a, b):
        return local(functools.partial(add_kernel, reach, tok), "add", 0, [vmem(a.shape, F32)], a, b)[0]

    sent = list(range(1, reach))
    first = pack([(m, 0) for m in sent])
    *second, own, own_first = pack([(m, 1) for m in sent] + [(0, 1), (0, 0)])
    packed = [[own_first, *first], [own, *second]]
    planes, before, after = [], [], []
    for c in range(CHUNKS):
        arrived = packed[c][:1] + [swapped(packed[c][m], "seq", m) for m in range(1, reach)]
        qd, kv = gather(c, arrived)
        planes.append((qd, kv))
        moved = passed_along(kv, "seq", reach), passed_along(qd, "seq", -reach)
        before.append(following(moved[0], moved[1]) if c == 0 else moved[0])
        after.append(moved[1])
    sums = jnp.zeros((8, tok), F32)
    pending, dqs, onehots = [], [], []
    for c in range(CHUNKS):
        *made, dq, dk, dv, stats, sums = rows_of(c, *planes[c], before[c], sums, *onehots)
        onehots = onehots or made
        dqs.append(dq)
        stats = passed_along(following(stats, after[c]), "seq", -reach)
        pending.append((after[c], planes[c][1], *onehots, stats, dk, dv))
    messages = [list(columns_of(0, *pending[0], *dqs))]
    messages.append(columns_of(1, *pending[1]))
    sums = following(sums, messages[0][0])
    mask = reach
    while mask < lax.axis_size("seq"):
        sums = add(sums, swapped(sums, "seq", mask))
        mask *= 2
    mask = 1
    while mask < lax.axis_size("dp"):
        sums = add(sums, swapped(sums, "dp", mask))
        mask *= 2
    out = [vmem((2 * tok + PAD, width))] * reach
    messages[1] = local(attach_kernel, "attach", 0, out, sums, *messages[1])
    parts = [[own[0]] + [swapped(own[m], "seq", m) for m in range(1, reach)] for own in messages]

    blocks = [((1, 0), (2, 0), (0, 0), (0, 1)), ((1, 1), (2, 1))]
    moves = [[(m, m, at, *to) for m in range(c, reach) for at, to in enumerate(blocks[c])] for c in range(CHUNKS)]
    moves[0] += [(reach, 0, at, *to) for at, to in enumerate(blocks[1])]
    parts[0].append(parts[1][0])
    grads = []
    for c in range(CHUNKS):
        last = c == CHUNKS - 1
        kernel = finish_kernel if last else unpack_kernel
        out = [jax.ShapeDtypeStruct((1, tok, row_width), BF16)] * 3
        grads = pl.pallas_call(
            functools.partial(kernel, reach, tok, group * HEAD_DIM, moves[c]),
            in_specs=[VMEM] * len(parts[c]) + [ANY] * len(grads),
            out_specs=[ANY] * (3 + last),
            out_shape=out + [jax.ShapeDtypeStruct((HEADS, FIELDS), F32)] * last,
            scratch_shapes=[pltpu.SemaphoreType.DMA((len(moves[c]),))]
            + [pltpu.VMEM((HEADS, FIELDS), F32), pltpu.SemaphoreType.DMA] * last,
            input_output_aliases={reach + at: at for at in range(len(grads))},
            compiler_params=params(2),
            cost_estimate=cost(0, 2 * MIB),
            name="unpack",
        )(*in_vmem(*parts[c]), *grads)
    return grads


def solution(mesh):
    return jax.shard_map(
        shards,
        mesh=mesh,
        in_specs=(
            P("dp", "seq", None),
            P("dp", "seq", None),
            P("dp", "seq", None),
            P("dp", "seq", None),
            P("dp"),
            P("dp", "seq"),
            P(),
        ),
        out_specs=(P("dp", "seq", None), P("dp", "seq", None), P("dp", "seq", None), P()),
        check_vma=False,
    )
```

```python
import functools

import jax
import jax.numpy as jnp
from jax import lax
from jax.experimental import pallas as pl
from jax.experimental.pallas import tpu as pltpu
from jax.sharding import PartitionSpec as P

HEADS = 16
HEAD_DIM = 128
WINDOW = 512
FIELDS = 64
FACTOR = HEAD_DIM ** (-0.5)
LOG2E = 1.4426950408889634
HIDDEN = -1e30
PAD = 16
CHUNKS = 2
MIB = 1 << 20
BF16, F32 = jnp.bfloat16, jnp.float32
ANY = pl.BlockSpec(memory_space=pl.ANY)
VMEM = pl.BlockSpec(memory_space=pltpu.VMEM)
GATHER_FLOPS, ROWS_FLOPS, COLUMNS_FLOPS = 2 * 10**9, 2 * 10**9, (4 * 10**9, 0)
NT = (((1,), (1,)), ((), ()))


def dot(a, b):
    return jnp.dot(a, b, preferred_element_type=F32)


def dot_nt(a, b):
    return lax.dot_general(a, b, NT, preferred_element_type=F32)


def place(reach):
    index = lax.axis_index("seq")
    return lax.rem(index, reach), lax.div(index, reach)


def pack_kernel(reach, tok, width, wanted, q, g, k, v, fields, *rest):
    outs, field_scr, sems = rest[: len(wanted)], rest[-2], rest[-1]
    p, _ = place(reach)
    field_copy = pltpu.make_async_copy(fields, field_scr, sems.at[4 * len(wanted)])
    field_copy.start()
    copies = []
    for out, (m, chunk) in zip(outs, wanted):
        first = pl.multiple_of((p ^ m) * (HEADS // reach * HEAD_DIM) + chunk * width, 128)
        for at, src in enumerate((q, g, k, v)):
            dst = out.at[pl.ds(at * tok, tok)]
            copies.append(pltpu.make_async_copy(src.at[0, :, pl.ds(first, width)], dst, sems.at[len(copies)]))
            copies[-1].start()
    field_copy.wait()
    row = jnp.concatenate([field_scr[...].astype(F32)] * (width // tok), axis=1)
    for out in outs:
        if out.shape[0] > 4 * tok:
            out[4 * tok :] = jnp.broadcast_to(row, (PAD, width)).astype(BF16)
    for copy in copies:
        copy.wait()


def gather_kernel(reach, tok, *refs):
    arrived, qd, kv = refs[:reach], *refs[reach:]
    for m in range(reach):
        qd[m] = arrived[m][: 2 * tok]
        kv[m] = arrived[m][2 * tok :]


def unpack_kernel(reach, tok, group_width, moves, *rest):
    outs, sems = rest[-4:-1], rest[-1]
    p, _ = place(reach)
    width = rest[0].shape[1]
    copies = []
    for i, m, at, which, chunk in moves:
        first = pl.multiple_of((p ^ m) * group_width + chunk * width, 128)
        dst = outs[which].at[0, :, pl.ds(first, width)]
        copies.append(pltpu.make_async_copy(rest[i].at[pl.ds(at * tok, tok)], dst, sems.at[len(copies)]))
        copies[-1].start()
    for copy in copies:
        copy.wait()


def finish_kernel(reach, tok, group_width, moves, *rest):
    total, sems, total_scr, total_sem = rest[-4:]
    join(reach, tok, 2 * tok, place(reach)[0], rest[:reach], total_scr)
    copy = pltpu.make_async_copy(total_scr, total, total_sem)
    copy.start()
    unpack_kernel(reach, tok, group_width, moves, *rest[:-4], sems)
    copy.wait()


def onehot_of(fields, slot, tok):
    row = fields[slot, 2 * tok : 2 * tok + PAD, 0:tok].astype(F32)[0:1]
    lane = lax.broadcasted_iota(jnp.int32, (tok, tok), 1)
    lane = jnp.where(lane < FIELDS, lane, lane - FIELDS).astype(F32)
    return jnp.where(jnp.broadcast_to(row, (tok, tok)).T == lane, 1.0, 0.0).astype(BF16)


def bias_columns(bias_ref, head, onehots):
    table = bias_ref[...].astype(F32)
    at = lax.broadcasted_iota(jnp.int32, table.shape, 0)
    row = jnp.sum(jnp.where(at == head, table, 0.0), axis=0, keepdims=True) * LOG2E
    row = jnp.concatenate([row, jnp.zeros_like(row)], axis=1)
    column = jnp.sum(onehots.astype(F32) * row, axis=1, keepdims=True)
    return jnp.broadcast_to(column, onehots.shape)


def three_parts(x):
    high = x.astype(BF16)
    rest = x - high.astype(F32)
    mid = rest.astype(BF16)
    return high, mid, (rest - mid.astype(F32)).astype(BF16)


def masks(tok):
    key_at = lax.broadcasted_iota(jnp.int32, (tok, tok), 0)
    query_at = lax.broadcasted_iota(jnp.int32, (tok, tok), 1)
    return key_at > query_at, lax.broadcasted_iota(jnp.int32, (1, tok), 1)


def query_pair(qd, p, a, tok, head):
    slots = (p ^ a, p ^ (a + 1))
    query = jnp.concatenate([qd[slot, 0:tok, head] for slot in slots], axis=0)
    grad = jnp.concatenate([qd[slot, tok : 2 * tok, head] for slot in slots], axis=0)
    return query, grad


def side_by_side(first, second, tok, ends):
    gap = jnp.zeros((tok, tok), first.dtype)
    first = jnp.concatenate([first, gap], axis=0) if ends else first
    return jnp.concatenate([first, jnp.concatenate([gap, second], axis=0)], axis=1)


def rows_kernel(reach, tok, chunk, lengths, qd, kvo, kvp, bias_ref, sums_in, *rest):
    *onehots, dq_out, dk_out, dv_out, stats_out, sums_out, k_scr, v_scr, kt_scr, acc_scr, bias_scr = rest
    onehots = onehots[0]
    p, plane = place(reach)
    length = lengths[...]
    span = reach * tok

    for blk in range(2 * reach):
        rows = slice(blk * tok, (blk + 1) * tok)
        if chunk == 0:
            onehots[rows] = onehot_of(kvp if blk < reach else kvo, p ^ (blk % reach), tok)
    per = kvo.shape[2] // HEAD_DIM
    sums_out[...] = sums_in[...]
    shut = jnp.where(plane == 0, HIDDEN, 0.0).astype(F32)
    later, lane = masks(tok)

    @pl.loop(0, kvo.shape[2] // HEAD_DIM, unroll=True)
    def _(h):
        head = pl.ds(pl.multiple_of(h * HEAD_DIM, HEAD_DIM), HEAD_DIM)
        at = chunk * per + h
        bias_scr[...] = bias_columns(bias_ref, p * (HEADS // reach) + at, onehots[...])
        for blk in range(2 * reach):
            rows = slice(blk * tok, (blk + 1) * tok)
            src, slot = (kvp if blk < reach else kvo), p ^ (blk % reach)
            key = src[slot, 0:tok, head]
            k_scr[rows] = key
            kt_scr[:, rows] = key.T
            v_scr[rows] = src[slot, tok : 2 * tok, head]
        acc_scr[...] = jnp.zeros_like(acc_scr)
        for pair in range(0, reach, 2):
            query, grad = query_pair(qd, p, pair, tok, head)
            wide = slice(pair * tok, (pair + reach + 2) * tok)
            logits = dot_nt(k_scr[wide], query)
            probs_both = dot_nt(v_scr[wide], grad)
            lows, ds_lows = [], []
            for half in range(2):
                a = pair + half
                rows = slice(a * tok, (a + reach + 1) * tok)
                mine = slice(half * tok, (half + reach + 1) * tok)
                there = slice(a * tok, (a + 1) * tok)
                cols = slice(half * tok, (half + 1) * tok)
                s = logits[mine, cols] * (FACTOR * LOG2E) + bias_scr[rows]
                seen = [jnp.where(later, s[:tok], HIDDEN) + shut, s[tok : (reach - a) * tok] + shut]
                seen += [s[(reach - a) * tok : -tok], jnp.where(later, HIDDEN, s[-tok:])]
                s = jnp.concatenate([part for part in seen if part.shape[0]], axis=0)
                peak = jnp.max(s, axis=0, keepdims=True)
                power = jnp.exp2(s - peak)
                total = jnp.sum(power, axis=0, keepdims=True)
                live = plane * span + a * tok + lane < length
                weight = power * jnp.where(live, 1.0 / total, 0.0)
                low = weight.astype(BF16)
                probs = probs_both[mine, cols]
                delta = jnp.sum(low.astype(F32) * probs, axis=0, keepdims=True)
                ds = weight * (probs - delta)
                acc_scr[rows] += ds
                lows.append(low)
                ds_lows.append(ds.astype(BF16))
                stats_out[h, 0:1, there] = peak + jnp.log2(total)
                stats_out[h, 1:2, there] = delta
            low = side_by_side(*lows, tok, True)
            ds_low = side_by_side(*ds_lows, tok, True)
            dq = dot(kt_scr[:, wide], ds_low)
            for half in range(2):
                dq_half = dq[:, half * tok : (half + 1) * tok]
                dq_out[p ^ (pair + half), :, head] = (dq_half.T * FACTOR).astype(BF16)
            own = slice((reach - pair) * tok, (reach + 2) * tok)
            dv = dot(low[own], grad)
            dk = dot(ds_low[own], query)
            done = pair * tok
            if pair:
                dv_out[0:done, head] += dv[:done]
                dk_out[0:done, head] += dk[:done]
            dv_out[done : done + 2 * tok, head] = dv[done:]
            dk_out[done : done + 2 * tok, head] = dk[done:]
        by_key = jnp.sum(acc_scr[...], axis=1, keepdims=True)
        row = jnp.sum(by_key * onehots[...].astype(F32), axis=0, keepdims=True)
        sums_out[...] += jnp.where(lax.broadcasted_iota(jnp.int32, (8, tok), 0) == at, row, 0.0)


def columns_kernel(reach, tok, chunk, lengths, qd, kvo, onehots, stats, bias_ref, dk_in, dv_in, *rest):
    k_scr, v_scr, dk_scr, dv_scr, bias_scr = rest[-5:]
    outs, extras = rest[-5 - reach : -5], rest[: -5 - reach]
    p, plane = place(reach)
    length = lengths[...]
    span = reach * tok
    later, lane = masks(tok)

    @pl.loop(0, kvo.shape[2] // HEAD_DIM, unroll=True)
    def _(h):
        head = pl.ds(pl.multiple_of(h * HEAD_DIM, HEAD_DIM), HEAD_DIM)
        at = chunk * (kvo.shape[2] // HEAD_DIM) + h
        bias_scr[...] = bias_columns(bias_ref, p * (HEADS // reach) + at, onehots[span:])
        for blk in range(reach):
            rows = slice(blk * tok, (blk + 1) * tok)
            k_scr[rows] = kvo[p ^ blk, 0:tok, head]
            v_scr[rows] = kvo[p ^ blk, tok : 2 * tok, head]
        for pair in range(0, reach, 2):
            query, grad = query_pair(qd, p, pair, tok, head)
            wide = slice(pair * tok, span)
            logits = dot_nt(k_scr[wide], query)
            probs_both = dot_nt(v_scr[wide], grad)
            lows, ds_lows = [], []
            for half in range(2):
                a = pair + half
                there = slice(a * tok, (a + 1) * tok)
                cols = slice(half * tok, (half + 1) * tok)
                live = (plane + 1) * span + a * tok + lane < length
                norm = jnp.where(live, stats[h, 0:1, there], -HIDDEN)
                delta = stats[h, 1:2, there]
                s = logits[half * tok :, cols] * (FACTOR * LOG2E) + bias_scr[a * tok :]
                weight = jnp.exp2(s - norm)
                first = jnp.where(later, weight[:tok], 0.0)
                weight = jnp.concatenate([first, weight[tok:]], axis=0) if a < reach - 1 else first
                lows.append(weight.astype(BF16))
                ds_lows.append((weight * (probs_both[half * tok :, cols] - delta)).astype(BF16))
            dv = dot(side_by_side(*lows, tok, False), grad)
            dk = dot(side_by_side(*ds_lows, tok, False), query)
            if pair:
                dv_scr[wide] += dv
                dk_scr[wide] += dk
            else:
                dv_scr[...] = dv + dv_in[:, head]
                dk_scr[...] = dk + dk_in[:, head]
        for m in range(reach):
            mine = pl.ds(pl.multiple_of((p ^ m) * tok, tok), tok)
            outs[m][0:tok, head] = (dk_scr[mine] * FACTOR).astype(BF16)
            outs[m][tok : 2 * tok, head] = dv_scr[mine].astype(BF16)
            for at, dq in enumerate(extras):
                outs[m][(2 + at) * tok : (3 + at) * tok, head] = dq[m, :, head]


def attach_kernel(sums, *refs):
    messages, outs = refs[: len(refs) // 2], refs[len(refs) // 2 :]
    parts = [part.astype(F32) for part in three_parts(sums[...])]
    parts = [jnp.concatenate(parts[:2], axis=1), jnp.concatenate([parts[2], jnp.zeros_like(parts[2])], axis=1)]
    below = jnp.concatenate(parts, axis=0).astype(BF16)
    for message, out in zip(messages, outs):
        count = message.shape[0]
        out[:count] = message[...]
        out[count:] = below


def add_kernel(reach, tok, a, b, out):
    out[...] = a[...] + b[...]


def join(reach, tok, first, p, slots, out):
    heads = HEADS // reach
    found = []
    for slot in slots:
        rows = slot[first : first + PAD].astype(F32)
        found.append(rows[:8, :FIELDS] + rows[:8, tok : tok + FIELDS] + rows[8:, :FIELDS])
    for q in range(reach):
        part = found[0]
        for m in range(1, reach):
            part = jnp.where(p == q ^ m, found[m], part)
        out[q * heads : (q + 1) * heads] = part[:heads]


def params(mib, *semantics):
    return pltpu.CompilerParams(
        vmem_limit_bytes=mib * MIB, dimension_semantics=semantics if semantics else None
    )


def cost(flops, nbytes, trans=0):
    return pl.CostEstimate(flops=flops, bytes_accessed=nbytes, transcendentals=trans)


def in_hbm(*arrays):
    return [pltpu.with_memory_space_constraint(array, pltpu.HBM) for array in arrays]


def in_vmem(*arrays):
    return [pltpu.with_memory_space_constraint(array, pltpu.VMEM) for array in arrays]


def following(value, mark):
    return lax.optimization_barrier((value, mark))[0]


def swapped(value, axis, mask):
    count = lax.axis_size(axis)
    return lax.ppermute(value, axis, [(source, source ^ mask) for source in range(count)])


def passed_along(value, axis, steps):
    count = lax.axis_size(axis)
    first, last = max(0, -steps), min(count, count - steps)
    return lax.ppermute(value, axis, [(source, source + steps) for source in range(first, last)])


def shards(queries, keys, values, grad_out, lengths, fields, field_bias):
    tok = queries.shape[1]
    row_width = queries.shape[2]
    reach = WINDOW // tok
    group = HEADS // reach
    per = group // CHUNKS
    width = per * HEAD_DIM
    span = reach * tok
    length = jnp.broadcast_to(lengths[:, None], (1, tok))
    raw = in_hbm(queries, grad_out, keys, values)

    def vmem(shape, dtype=BF16):
        return pltpu.VMEM(shape, dtype)


    def pad(chunk):
        return 0 if chunk else PAD

    def pack(wanted):
        return pl.pallas_call(
            functools.partial(pack_kernel, reach, tok, width, wanted),
            in_specs=[ANY] * 5,
            out_specs=[VMEM] * len(wanted),
            out_shape=[vmem((4 * tok + pad(chunk), width)) for _, chunk in wanted],
            scratch_shapes=[
                pltpu.VMEM((1, tok), jnp.int32),
                pltpu.SemaphoreType.DMA((4 * len(wanted) + 1,)),
            ],
            compiler_params=params(2),
            cost_estimate=cost(0, 2 * MIB),
            name="pack",
        )(*raw, *in_hbm(fields))

    def local(kernel, name, flops, out_shape, *args, scratch=()):
        return pl.pallas_call(
            kernel,
            in_specs=[VMEM] * len(args),
            out_specs=[VMEM] * len(out_shape),
            out_shape=out_shape,
            scratch_shapes=scratch,
            compiler_params=params(12),
            cost_estimate=cost(flops, 2 * MIB),
            name=name,
        )(*in_vmem(*args))

    def gather(chunk, arrived):
        out = [vmem((reach, 2 * tok, width)), vmem((reach, 2 * tok + pad(chunk), width))]
        return local(functools.partial(gather_kernel, reach, tok), "gather", GATHER_FLOPS if chunk else 0, out, *arrived)

    def rows_of(chunk, qd, kvo, kvp, sums, *onehots):
        out = [
            vmem((reach, tok, width)),
            vmem((span, width), F32),
            vmem((span, width), F32),
            vmem((per, 2, span), F32),
            vmem((8, tok), F32),
        ]
        if chunk == 0:
            out = [vmem((2 * span, tok))] + out
        scratch = [
            pltpu.VMEM((2 * span, HEAD_DIM), BF16),
            pltpu.VMEM((2 * span, HEAD_DIM), BF16),
            pltpu.VMEM((HEAD_DIM, 2 * span), BF16),
            pltpu.VMEM((2 * span, tok), F32),
            pltpu.VMEM((2 * span, tok), F32),
        ]
        kernel = functools.partial(rows_kernel, reach, tok, chunk)
        args = (length, qd, kvo, kvp, field_bias, sums, *onehots)
        return local(kernel, "rows", ROWS_FLOPS, out, *args, scratch=scratch)

    def columns_of(chunk, qd, kvo, onehots, stats, dk, dv, *extras):
        out = [vmem(((2 + len(extras)) * tok, width))] * reach
        scratch = [
            pltpu.VMEM((span, HEAD_DIM), BF16),
            pltpu.VMEM((span, HEAD_DIM), BF16),
            pltpu.VMEM((span, HEAD_DIM), F32),
            pltpu.VMEM((span, HEAD_DIM), F32),
            pltpu.VMEM((span, tok), F32),
        ]
        kernel = functools.partial(columns_kernel, reach, tok, chunk)
        args = (length, qd, kvo, onehots, stats, field_bias, dk, dv, *extras)
        return local(kernel, "columns", COLUMNS_FLOPS[chunk], out, *args, scratch=scratch)

    def add(a, b):
        return local(functools.partial(add_kernel, reach, tok), "add", 0, [vmem(a.shape, F32)], a, b)[0]

    sent = list(range(1, reach))
    first = pack([(m, 0) for m in sent])
    *second, own, own_first = pack([(m, 1) for m in sent] + [(0, 1), (0, 0)])
    packed = [[own_first, *first], [own, *second]]
    planes, before, after = [], [], []
    for c in range(CHUNKS):
        arrived = packed[c][:1] + [swapped(packed[c][m], "seq", m) for m in range(1, reach)]
        qd, kv = gather(c, arrived)
        planes.append((qd, kv))
        moved = passed_along(kv, "seq", reach), passed_along(qd, "seq", -reach)
        before.append(following(moved[0], moved[1]) if c == 0 else moved[0])
        after.append(moved[1])
    sums = jnp.zeros((8, tok), F32)
    pending, dqs, onehots = [], [], []
    for c in range(CHUNKS):
        *made, dq, dk, dv, stats, sums = rows_of(c, *planes[c], before[c], sums, *onehots)
        onehots = onehots or made
        dqs.append(dq)
        stats = passed_along(following(stats, after[c]), "seq", -reach)
        pending.append((after[c], planes[c][1], *onehots, stats, dk, dv))
    messages = [list(columns_of(0, *pending[0], *dqs))]
    messages.append(columns_of(1, *pending[1]))
    sums = following(sums, messages[0][0])
    mask = reach
    while mask < lax.axis_size("seq"):
        sums = add(sums, swapped(sums, "seq", mask))
        mask *= 2
    mask = 1
    while mask < lax.axis_size("dp"):
        sums = add(sums, swapped(sums, "dp", mask))
        mask *= 2
    out = [vmem((2 * tok + PAD, width))] * reach
    messages[1] = local(attach_kernel, "attach", 0, out, sums, *messages[1])
    parts = [[own[0]] + [swapped(own[m], "seq", m) for m in range(1, reach)] for own in messages]

    blocks = [((1, 0), (2, 0), (0, 0), (0, 1)), ((1, 1), (2, 1))]
    moves = [[(m, m, at, *to) for m in range(c, reach) for at, to in enumerate(blocks[c])] for c in range(CHUNKS)]
    moves[0] += [(reach, 0, at, *to) for at, to in enumerate(blocks[1])]
    parts[0].append(parts[1][0])
    grads = []
    for c in range(CHUNKS):
        last = c == CHUNKS - 1
        kernel = finish_kernel if last else unpack_kernel
        out = [jax.ShapeDtypeStruct((1, tok, row_width), BF16)] * 3
        grads = pl.pallas_call(
            functools.partial(kernel, reach, tok, group * HEAD_DIM, moves[c]),
            in_specs=[VMEM] * len(parts[c]) + [ANY] * len(grads),
            out_specs=[ANY] * (3 + last),
            out_shape=out + [jax.ShapeDtypeStruct((HEADS, FIELDS), F32)] * last,
            scratch_shapes=[pltpu.SemaphoreType.DMA((len(moves[c]),))]
            + [pltpu.VMEM((HEADS, FIELDS), F32), pltpu.SemaphoreType.DMA] * last,
            input_output_aliases={reach + at: at for at in range(len(grads))},
            compiler_params=params(2),
            cost_estimate=cost(0, 2 * MIB),
            name="unpack",
        )(*in_vmem(*parts[c]), *grads)
    return grads


def solution(mesh):
    return jax.shard_map(
        shards,
        mesh=mesh,
        in_specs=(
            P("dp", "seq", None),
            P("dp", "seq", None),
            P("dp", "seq", None),
            P("dp", "seq", None),
            P("dp"),
            P("dp", "seq"),
            P(),
        ),
        out_specs=(P("dp", "seq", None), P("dp", "seq", None), P("dp", "seq", None), P()),
        check_vma=False,
    )
```
